768 devices in a mesh: proto: 24 (over z, core), batch: 32 (over y, x).
Axes of the slice: x: 4, y: 8, z: 12, core: 2. Of those that a mesh axis runs over, the one named last changes fastest.
Arguments:
- teacher: bfloat16 [8192, 256], P('batch'), may hold values from -6 to 6
- student: bfloat16 [8192, 256], P('batch'), may hold values from -6 to 6
- prototypes: bfloat16 [256, 67584], P(None, 'proto'), may hold values from -0.375 to 0.375
- gain: float32 [67584], P('proto'), may hold values from 1 to 2.5
Outputs:
- targets: bfloat16 [8192, 67584], P('batch', 'proto')
- prototype_grad: float32 [256, 67584], P('batch', 'proto')
The draws below stay inside these ranges and needn't reach their ends.
All inputs are finite; a program needn't handle non-finite values.
Results may differ from the reference program's by a relative error of at most 0.01.
The reference program's roundings to bfloat16 on the way (of `proto_n`, `teacher_n`, `expo` and `diff`) count: a program that leaves them out, or rounds other values in their place, can miss the bound.
Values sent between devices are 32-bit elements; how exact they have to be, the bound alone decides.
No kernel may reach another device: no remote copies, remote signals or barrier semaphores. Data moves between devices by JAX's collectives and lax.ppermute only.
A program may use at most 32 MiB of HBM per device.

```python
import math
import jax
import jax.numpy as jnp
from jax import lax

D = 256
ITERS = 3
K = 67584
ROWS = 8192


def shard_levels(stream_key, shape, shards, low, high):
    factor_of = 1.0
    for position, blocks in shards:
        steps = jax.random.uniform(jax.random.fold_in(jax.random.fold_in(stream_key, 6), position), (blocks,), jnp.float32, low / len(shards), high / len(shards))
        factor_of = factor_of * jnp.repeat(jnp.exp(steps), shape[position] // blocks).reshape((-1,) + (1,) * (len(shape) - 1 - position))
    return factor_of


def normal_values(own_key, shape, deviation, limit, cuts=(), dtype=jnp.bfloat16):
    factor_of = shard_levels(own_key, shape, cuts, -0.22, 0.18) if cuts else 1.0
    entries = jax.random.normal(own_key, shape, jnp.float32) * deviation * factor_of
    return jnp.minimum(jnp.maximum(entries, -limit), limit).astype(dtype)


def setup_inputs(seed: int = 0) -> dict:
    key_of = jax.random.split(jax.random.key(seed), 5)
    return {
        "teacher": normal_values(key_of[0], (ROWS, D), 1.0, 6.0, ((0, 32),)),
        "student": normal_values(key_of[1], (ROWS, D), 1.0, 6.0, ((0, 32),)),
        "prototypes": normal_values(key_of[2], (D, K), D ** -0.5, 0.375, ((1, 24),)),
        "gain": jnp.clip(jnp.exp(math.log(2.5) - 0.916290732 * jax.random.uniform(key_of[3], (K,), jnp.float32) ** shard_levels(key_of[3], (K,), ((0, 24),), -0.2, 0.2)), 1.0, 2.5),
    }


teacher_temp = 0.04
student_temp = 0.1
eps = 1e-06

def unit_rows(x):
    xf = x.astype(jnp.float32)
    return (xf * lax.rsqrt(lax.optimization_barrier(jnp.sum(xf * xf, 1, keepdims=True)) + eps)).astype(jnp.bfloat16)

def reference(teacher, student, prototypes, gain):
    rows = teacher.shape[0]
    block = math.gcd(rows, 512)
    nblk = rows // block
    wf = prototypes.astype(jnp.float32)
    proto_n = (wf * lax.rsqrt(lax.optimization_barrier(jnp.sum(wf * wf, 0, keepdims=True)) + eps) * gain[None, :]).astype(jnp.bfloat16)
    count = proto_n.shape[1]
    teacher_n = unit_rows(teacher).reshape(nblk, block, -1)
    student_n = unit_rows(student).reshape(nblk, block, -1)

    def expo(rows_b):
        value = jnp.exp(jnp.dot(rows_b, proto_n, preferred_element_type=jnp.float32) / teacher_temp).astype(jnp.bfloat16)
        return lax.optimization_barrier(value).astype(jnp.float32)
    scale_v = jnp.ones((nblk, block), jnp.float32)
    scale_u = jnp.ones((count,), jnp.float32)
    for step in range(ITERS):
        partial_c = lax.map(lambda pair: jnp.dot(pair[1], expo(pair[0]), precision=lax.Precision.HIGHEST), (teacher_n, scale_v))
        scale_u = 1.0 / lax.optimization_barrier(jnp.sum(partial_c, 0))
        row_tot = lax.map(lambda rows_b: jnp.dot(expo(rows_b), scale_u, precision=lax.Precision.HIGHEST), teacher_n)
        scale_v = 1.0 / row_tot

    def final(carry, items):
        rows_t, rows_s, vblock = items
        assign = expo(rows_t) * scale_u[None, :] * vblock[:, None]
        targets = (count * assign).astype(jnp.bfloat16)
        logits = jnp.dot(rows_s, proto_n, preferred_element_type=jnp.float32) / student_temp
        total = lax.optimization_barrier(jnp.sum(jnp.exp(logits), 1, keepdims=True))
        prob = jnp.exp(logits - jnp.log(total))
        diff = (count * (prob - assign)).astype(jnp.bfloat16)
        return (carry + jnp.dot(rows_s.T, diff, preferred_element_type=jnp.float32), targets)
    init = jnp.zeros((proto_n.shape[0], count), jnp.float32)
    grad, targets = lax.scan(final, init, (teacher_n, student_n, scale_v))
    grad = grad / jnp.sqrt(jnp.float32(rows))
    return (targets.reshape(rows, count), grad)
```

```python
import jax
import jax.numpy as jnp
from jax import lax
from jax.sharding import PartitionSpec as P

ITERS = 3
NX = 4


teacher_temp = 0.04
student_temp = 0.1
eps = 1e-06


def unit_rows(x):
    xf = x.astype(jnp.float32)
    return (xf * lax.rsqrt(jnp.sum(xf * xf, 1, keepdims=True) + eps)).astype(jnp.bfloat16)


def spread_sum(value, axis):
    n = lax.axis_size(axis)
    sent = jnp.broadcast_to(value[None], (n,) + value.shape)
    return jnp.sum(lax.all_to_all(sent, axis, 0, 0, tiled=True), 0)


def local(teacher, student, prototypes, gain):
    rows, depth = teacher.shape
    nb, npr = lax.axis_size("batch"), lax.axis_size("proto")
    ny = nb // NX
    x_groups = [[y * NX + x for x in range(NX)] for y in range(ny)]
    xp_groups = [[b * npr + p for b in group for p in range(npr)] for group in x_groups]
    x_me = lax.axis_index("batch") % NX

    both = jnp.concatenate([teacher, student], 0).astype(jnp.float32)
    both = lax.optimization_barrier(both)
    gathered = lax.all_gather(both, "batch", axis_index_groups=x_groups)

    wf = prototypes.astype(jnp.float32)
    proto_n = (wf * lax.rsqrt(jnp.sum(wf * wf, 0, keepdims=True) + eps) * gain[None, :]).astype(
        jnp.bfloat16
    )
    cols = proto_n.shape[1]
    part = cols // NX
    count = cols * npr
    rows_all = rows * nb
    teacher_n = unit_rows(teacher)
    student_n = unit_rows(student)
    expo = jnp.exp(
        jnp.dot(teacher_n, proto_n, preferred_element_type=jnp.float32) / teacher_temp
    ).astype(jnp.bfloat16)
    expo_wide = lax.optimization_barrier(expo).astype(jnp.float32)
    logits = jnp.dot(student_n, proto_n, preferred_element_type=jnp.float32) / student_temp
    local_total = jnp.sum(jnp.exp(logits), 1)

    teacher_x = unit_rows(gathered[:, :rows].reshape(NX * rows, depth))
    student_x = unit_rows(gathered[:, rows:].reshape(NX * rows, depth))
    proto_x = lax.dynamic_slice_in_dim(proto_n, x_me * part, part, 1)
    expo_x = jnp.exp(
        jnp.dot(teacher_x, proto_x, preferred_element_type=jnp.float32) / teacher_temp
    ).astype(jnp.bfloat16)
    expo_x = lax.optimization_barrier(expo_x)
    logits_x = jnp.dot(student_x, proto_x, preferred_element_type=jnp.float32) / student_temp

    scale_v = jnp.ones((rows,), jnp.float32)
    for step in range(ITERS):
        scale_u = 1.0 / spread_sum(
            jnp.dot(scale_v, expo_wide, precision=lax.Precision.HIGHEST), "batch"
        )
        partial_r = jnp.dot(expo_wide, scale_u, precision=lax.Precision.HIGHEST)
        if step + 1 < ITERS:
            scale_v = 1.0 / spread_sum(partial_r, "proto")
    sent = jnp.stack([partial_r, local_total])
    sent = jnp.broadcast_to(sent[None], (NX * npr, 2, rows))
    came = lax.all_to_all(
        sent, ("batch", "proto"), 0, 0, tiled=True, axis_index_groups=xp_groups
    ).reshape(NX, npr, 2, rows)
    tot = jnp.sum(came, 1)
    scale_v_x = 1.0 / tot[:, 0].reshape(-1)
    total_x = tot[:, 1].reshape(-1)
    scale_v = lax.dynamic_index_in_dim(1.0 / tot[:, 0], x_me, 0, keepdims=False)
    scale_u_x = lax.dynamic_slice_in_dim(scale_u, x_me * part, part, 0)

    assign_x = expo_x.astype(jnp.float32) * scale_u_x[None, :] * scale_v_x[:, None]
    prob_x = jnp.exp(logits_x - jnp.log(total_x)[:, None])
    diff_x = (count * (prob_x - assign_x)).astype(jnp.bfloat16)
    inv_root = 1.0 / jnp.sqrt(jnp.float32(rows_all))
    grad_x = jnp.dot(student_x.T, diff_x, preferred_element_type=jnp.float32) * inv_root
    own = depth // nb
    parts = lax.all_to_all(grad_x.reshape(nb, own, part), "batch", 0, 0, tiled=True)
    grad = jnp.sum(parts.reshape(ny, NX, own, part), 0)
    grad = jnp.swapaxes(grad, 0, 1).reshape(own, cols)

    assign = expo_wide * scale_u[None, :] * scale_v[:, None]
    targets = (count * assign).astype(jnp.bfloat16)
    return (targets, grad)


def solution(mesh):
    return jax.shard_map(
        local,
        mesh=mesh,
        in_specs=(P("batch", None), P("batch", None), P(None, "proto"), P("proto")),
        out_specs=(P("batch", "proto"), P("batch", "proto")),
        check_vma=False,
    )
```

```python
import functools

import jax
import jax.numpy as jnp
from jax import lax
from jax.experimental import pallas as pl
from jax.experimental.pallas import tpu as pltpu
from jax.sharding import PartitionSpec as P

ITERS = 3
TEAM = 8


teacher_temp = 0.04
student_temp = 0.1
eps = 1e-06


def unit_rows(x):
    xf = x.astype(jnp.float32)
    return (xf * lax.rsqrt(jnp.sum(xf * xf, 1, keepdims=True) + eps)).astype(jnp.bfloat16)


def spread(value, axis, size, groups=None):
    sent = jnp.broadcast_to(value[None], (size,) + value.shape)
    return lax.all_to_all(sent, axis, 0, 0, tiled=True, axis_index_groups=groups)


def grad_kernel(count, scale, expo_ref, student_exp_ref, student_ref, u_ref, rows_ref, out_ref, acc):
    step = pl.program_id(0)

    @pl.when(step == 0)
    def _():
        acc[...] = jnp.zeros_like(acc)

    rows = rows_ref.shape[2]
    u = u_ref[...]
    for s in range(rows_ref.shape[0]):
        span = slice(s * rows, (s + 1) * rows)
        v = rows_ref[s, 0:1, :]
        inv_total = rows_ref[s, 1:2, :]
        assign = expo_ref[:, span].astype(jnp.float32) * u * v
        diff = (count * (student_exp_ref[:, span] * inv_total - assign)).astype(jnp.bfloat16)
        acc[...] += jnp.dot(diff, student_ref[span, :], preferred_element_type=jnp.float32)

    @pl.when(step == pl.num_programs(0) - 1)
    def _():
        out_ref[...] = (acc[...].T * scale).reshape(out_ref.shape)


def partial_grad(expo_t, student_exp_t, student, u, by_sender, count, scale, owners):
    part, crops = expo_t.shape
    depth = student.shape[1]
    senders, _, rows = by_sender.shape
    steps = 4
    chunk = crops // steps
    return pl.pallas_call(
        functools.partial(grad_kernel, count, scale),
        grid=(steps,),
        in_specs=[
            pl.BlockSpec((part, chunk), lambda i: (0, i)),
            pl.BlockSpec((part, chunk), lambda i: (0, i)),
            pl.BlockSpec((chunk, depth), lambda i: (i, 0)),
            pl.BlockSpec((part, 1), lambda i: (0, 0)),
            pl.BlockSpec((senders // steps, 2, rows), lambda i: (i, 0, 0)),
        ],
        out_specs=pl.BlockSpec((owners, depth // owners, part), lambda i: (0, 0, 0)),
        out_shape=jax.ShapeDtypeStruct((owners, depth // owners, part), jnp.float32),
        scratch_shapes=[pltpu.VMEM((part, depth), jnp.float32)],
        compiler_params=pltpu.CompilerParams(vmem_limit_bytes=24 * 1024 * 1024),
        cost_estimate=pl.CostEstimate(
            flops=2 * part * crops * depth, bytes_accessed=6 * part * crops, transcendentals=0
        ),
    )(expo_t, student_exp_t, student, u, by_sender)


def local(teacher, student, prototypes, gain):
    rows, depth = teacher.shape
    nb, npr = lax.axis_size("batch"), lax.axis_size("proto")
    teams = [[t * TEAM + i for i in range(TEAM)] for t in range(nb // TEAM)]
    me = lax.axis_index("batch") % TEAM

    both = jnp.concatenate([teacher, student], 0).astype(jnp.float32)
    both = lax.optimization_barrier(both)
    gathered = lax.all_gather(both, "batch", axis_index_groups=teams)

    wf = prototypes.astype(jnp.float32)
    proto_n = (wf * lax.rsqrt(jnp.sum(wf * wf, 0, keepdims=True) + eps) * gain[None, :]).astype(
        jnp.bfloat16
    )
    cols = proto_n.shape[1]
    part = cols // TEAM
    count = cols * npr
    rows_all = rows * nb
    teacher_n = unit_rows(teacher)
    expo = jnp.exp(
        jnp.dot(teacher_n, proto_n, preferred_element_type=jnp.float32) / teacher_temp
    ).astype(jnp.bfloat16)
    expo_wide = lax.optimization_barrier(expo).astype(jnp.float32)

    scale_v = jnp.ones((rows,), jnp.float32)
    for step in range(ITERS):
        last = step + 1 == ITERS
        if last:
            scale_v, gathered, student, proto_n = lax.optimization_barrier(
                (scale_v, gathered, student, proto_n)
            )
        c = jnp.dot(scale_v, expo_wide, precision=lax.Precision.HIGHEST)
        scale_u = 1.0 / jnp.sum(spread(c, "batch", nb), 0)
        partial_r = jnp.dot(expo_wide, scale_u, precision=lax.Precision.HIGHEST)
        if not last:
            scale_v = 1.0 / jnp.sum(spread(partial_r, "proto", npr), 0)

    logits = jnp.dot(unit_rows(student), proto_n, preferred_element_type=jnp.float32)
    local_total = jnp.sum(jnp.exp(logits / student_temp), 1)
    teacher_t = unit_rows(gathered[:, :rows].reshape(TEAM * rows, depth))
    student_t = unit_rows(gathered[:, rows:].reshape(TEAM * rows, depth))
    proto_t = lax.dynamic_slice_in_dim(proto_n, me * part, part, 1)
    across = (((0,), (1,)), ((), ()))
    expo_t = jnp.exp(
        lax.dot_general(proto_t, teacher_t, across, preferred_element_type=jnp.float32)
        / teacher_temp
    ).astype(jnp.bfloat16)
    student_exp_t = jnp.exp(
        lax.dot_general(proto_t, student_t, across, preferred_element_type=jnp.float32)
        / student_temp
    )
    u_t = lax.dynamic_slice_in_dim(scale_u, me * part, part, 0)[:, None]
    sent = jnp.stack([partial_r, local_total])
    sent, expo_t, student_exp_t, student_t, u_t = lax.optimization_barrier(
        (sent, expo_t, student_exp_t, student_t, u_t)
    )
    inverse = 1.0 / jnp.sum(spread(sent, "proto", npr), 0)
    scale_v = inverse[0]
    by_sender = spread(inverse, "batch", TEAM, teams)

    inv_root = 1.0 / rows_all**0.5
    grad_t = partial_grad(
        expo_t, student_exp_t, student_t, u_t, by_sender, float(count), inv_root, nb
    )
    parts = lax.all_to_all(grad_t, "batch", 0, 0, tiled=True)
    own = depth // nb
    grad = jnp.sum(parts.reshape(nb // TEAM, TEAM, own, part), 0)
    grad = jnp.swapaxes(grad, 0, 1).reshape(own, cols)

    assign = expo_wide * scale_u[None, :] * scale_v[:, None]
    targets = (count * assign).astype(jnp.bfloat16)
    return (targets, grad)


def solution(mesh):
    return jax.shard_map(
        local,
        mesh=mesh,
        in_specs=(P("batch", None), P("batch", None), P(None, "proto"), P("proto")),
        out_specs=(P("batch", "proto"), P("batch", "proto")),
        check_vma=False,
    )
```

```python
import functools

import jax
import jax.numpy as jnp
from jax import lax
from jax.experimental import pallas as pl
from jax.experimental.pallas import tpu as pltpu
from jax.sharding import PartitionSpec as P

ITERS = 3
SMALL, PASSING, VMEM = 16 * 2**20, 121 * 2**19, 61 * 2**20
LANES = 128
HELD = 3
TEAM = 8


teacher_temp = 0.04
student_temp = 0.1
eps = 1e-06


def unit_rows(x):
    xf = x.astype(jnp.float32)
    return (xf * lax.rsqrt(jnp.sum(xf * xf, 1, keepdims=True) + eps)).astype(jnp.bfloat16)


def spread(value, axis, size, groups=None):
    sent = jnp.broadcast_to(value[None], (size,) + value.shape)
    return lax.all_to_all(sent, axis, 0, 0, tiled=True, axis_index_groups=groups)


def first_group(groups):
    return jnp.minimum(lax.axis_index("batch") % TEAM * HELD, groups - HELD)


def grad_kernel(count, scale, expo_ref, student_exp_ref, student_ref, u_ref, rows_ref, out_ref, acc, u_wide):
    step = pl.program_id(0)

    @pl.when(step == 0)
    def _():
        acc[...] = jnp.zeros_like(acc)
        u = u_ref[pl.ds(first_group(u_ref.shape[0]), HELD), :]
        for g in range(HELD):
            wide = jnp.broadcast_to(u[g : g + 1, :], (LANES, LANES)).T
            u_wide[g * LANES : (g + 1) * LANES, :] = wide

    rows = rows_ref.shape[2]
    u = u_wide[...]
    for s in range(rows_ref.shape[0]):
        for start in range(0, rows, LANES):
            v = rows_ref[s, 0:1, start : start + LANES]
            inv_total = rows_ref[s, 1:2, start : start + LANES]
            span = slice(s * rows + start, s * rows + start + LANES)
            assign = expo_ref[:, span].astype(jnp.float32) * u * v
            diff = count * (student_exp_ref[:, span] * inv_total - assign)
            acc[...] += jnp.dot(
                diff.astype(jnp.bfloat16), student_ref[span, :], preferred_element_type=jnp.float32
            )

    @pl.when(step == pl.num_programs(0) - 1)
    def _():
        out_ref[...] = (acc[...].T * scale).reshape(out_ref.shape)


def partial_grad(expo_t, student_exp_t, student, u, by_sender, count, scale, owners):
    part, crops = expo_t.shape
    depth = student.shape[1]
    senders, _, rows = by_sender.shape
    steps = 4
    chunk = crops // steps
    return pl.pallas_call(
        functools.partial(grad_kernel, count, scale),
        grid=(steps,),
        in_specs=[
            pl.BlockSpec((part, chunk), lambda i: (0, i)),
            pl.BlockSpec((part, chunk), lambda i: (0, i)),
            pl.BlockSpec((chunk, depth), lambda i: (i, 0)),
            pl.BlockSpec(u.shape, lambda i: (0, 0)),
            pl.BlockSpec((senders // steps, 2, rows), lambda i: (i, 0, 0)),
        ],
        out_specs=pl.BlockSpec((owners, depth // owners, part), lambda i: (0, 0, 0)),
        out_shape=jax.ShapeDtypeStruct((owners, depth // owners, part), jnp.float32),
        scratch_shapes=[
            pltpu.VMEM((part, depth), jnp.float32),
            pltpu.VMEM((part, LANES), jnp.float32),
        ],
        compiler_params=pltpu.CompilerParams(vmem_limit_bytes=VMEM),
        cost_estimate=pl.CostEstimate(
            flops=2 * part * crops * depth, bytes_accessed=6 * part * crops, transcendentals=0
        ),
    )(expo_t, student_exp_t, student, u, by_sender)


def join_kernel(parts_ref, out_ref):
    teams = parts_ref.shape[0] // TEAM
    groups = out_ref.shape[1] // LANES
    for i in range(TEAM):
        start = min(i * HELD, groups - HELD) * LANES
        total = parts_ref[i]
        for t in range(1, teams):
            total += parts_ref[t * TEAM + i]
        out_ref[:, start : start + HELD * LANES] = total


def row_kernel(came_ref, expo_ref, *refs):
    total_ref, (sent_ref, u_ref) = (refs[0] if len(refs) == 3 else None), refs[-2:]
    u_ref[...] = 1.0 / jnp.sum(came_ref[...], 0)
    rows = expo_ref.shape[0]
    block = 64
    sums = []
    for start in range(0, rows, block):
        acc = jnp.zeros((block, LANES), jnp.float32)
        for j in range(u_ref.shape[0]):
            e = expo_ref[start : start + block, j * LANES : (j + 1) * LANES].astype(jnp.float32)
            acc += e * u_ref[j : j + 1, :]
        sums.append(acc)
    r = jnp.sum(jnp.concatenate(sums, 0).T, 0, keepdims=True)
    peers = sent_ref.shape[0]
    sent_ref[:, 0:1, :] = jnp.broadcast_to(r[None], (peers, 1, rows))
    if total_ref is not None:
        sent_ref[:, 1:2, :] = jnp.broadcast_to(total_ref[...][None], (peers, 1, rows))


def row_terms(came, expo, peers, total=None):
    more = () if total is None else (total,)
    _, groups, _ = came.shape
    rows = expo.shape[0]
    return pl.pallas_call(
        row_kernel,
        out_shape=(
            jax.ShapeDtypeStruct((peers, 1 + len(more), rows), jnp.float32),
            jax.ShapeDtypeStruct((groups, LANES), jnp.float32),
        ),
        compiler_params=pltpu.CompilerParams(vmem_limit_bytes=SMALL),
        cost_estimate=pl.CostEstimate(flops=2 * expo.size, bytes_accessed=2 * expo.size, transcendentals=0),
    )(came, expo, *more)


def column_kernel(came_ref, expo_ref, *refs):
    sent_ref = refs[len(refs) // 2]
    rows = expo_ref.shape[0]
    v = 1.0 / jnp.sum(came_ref[...], 0)
    v = jnp.broadcast_to(v, (LANES, rows)).T
    peers, groups, _ = sent_ref.shape
    for j in range(groups):
        e = expo_ref[:, j * LANES : (j + 1) * LANES].astype(jnp.float32)
        sent_ref[0, j : j + 1, :] = jnp.sum(e * v, 0, keepdims=True)
    sent_ref[1:] = jnp.broadcast_to(sent_ref[0:1], (peers - 1, groups, LANES))


def column_terms(came, expo, peers, passed=None):
    groups = expo.shape[1] // LANES
    more = () if passed is None else (passed,)
    out = pl.pallas_call(
        column_kernel,
        in_specs=[pl.BlockSpec(), pl.BlockSpec()] + [pl.BlockSpec(memory_space=pl.ANY)] * len(more),
        out_specs=[pl.BlockSpec()] + [pl.BlockSpec(memory_space=pl.ANY)] * len(more),
        out_shape=[jax.ShapeDtypeStruct((peers, groups, LANES), jnp.float32)]
        + [jax.ShapeDtypeStruct(m.shape, m.dtype) for m in more],
        input_output_aliases={2: 1} if more else {},
        compiler_params=pltpu.CompilerParams(vmem_limit_bytes=PASSING if more else SMALL),
        cost_estimate=pl.CostEstimate(flops=2 * expo.size, bytes_accessed=2 * expo.size, transcendentals=0),
    )(came, expo, *more)
    return out if more else out[0]


def team_kernel(rows_ref, proto_ref, after_ref, expo_ref, student_exp_ref, student_ref, proto_t):
    @pl.when(pl.program_id(0) == 0)
    def _():
        start = pl.multiple_of(first_group(proto_ref.shape[1] // LANES) * LANES, LANES)
        proto_t[...] = proto_ref[:, pl.ds(start, HELD * LANES)].astype(jnp.float32).T.astype(jnp.bfloat16)

    def unit(x):
        return (x * lax.rsqrt(jnp.sum(x * x, 1, keepdims=True) + eps)).astype(jnp.bfloat16)

    across = (((1,), (1,)), ((), ()))
    proto = proto_t[...]
    t = unit(rows_ref[0, 0])
    s = unit(rows_ref[1, 0])
    student_ref[...] = s
    lt = lax.dot_general(proto, t, across, preferred_element_type=jnp.float32)
    expo_ref[...] = jnp.exp(lt / teacher_temp).astype(jnp.bfloat16)
    ls = lax.dot_general(proto, s, across, preferred_element_type=jnp.float32)
    student_exp_ref[...] = jnp.exp(ls / student_temp)


def team_products(gathered, proto, after):
    _, senders, rows, depth = gathered.shape
    part = HELD * LANES
    return pl.pallas_call(
        team_kernel,
        grid=(senders,),
        in_specs=[
            pl.BlockSpec((2, 1, rows, depth), lambda i: (0, i, 0, 0)),
            pl.BlockSpec(proto.shape, lambda i: (0, 0)),
            pl.BlockSpec(memory_space=pl.ANY),
        ],
        out_specs=[
            pl.BlockSpec((part, rows), lambda i: (0, i)),
            pl.BlockSpec((part, rows), lambda i: (0, i)),
            pl.BlockSpec((rows, depth), lambda i: (i, 0)),
        ],
        out_shape=(
            jax.ShapeDtypeStruct((part, senders * rows), jnp.bfloat16),
            jax.ShapeDtypeStruct((part, senders * rows), jnp.float32),
            jax.ShapeDtypeStruct((senders * rows, depth), jnp.bfloat16),
        ),
        scratch_shapes=[pltpu.VMEM((part, depth), jnp.bfloat16)],
        compiler_params=pltpu.CompilerParams(vmem_limit_bytes=VMEM),
        cost_estimate=pl.CostEstimate(
            flops=4 * part * senders * rows * depth,
            bytes_accessed=10 * 2**20,
            transcendentals=2 * part * senders * rows,
        ),
    )(gathered, proto, after)


def local(teacher, student, prototypes, gain):
    rows, depth = teacher.shape
    nb, npr = lax.axis_size("batch"), lax.axis_size("proto")
    teams = [[t * TEAM + i for i in range(TEAM)] for t in range(nb // TEAM)]
    chips = [[2 * z, 2 * z + 1] for z in range(npr // 2)]
    core = lax.axis_index("proto") % 2

    mine = jnp.where(core == 0, teacher.astype(jnp.float32), student.astype(jnp.float32))
    mine = lax.optimization_barrier(mine)
    gathered = lax.all_gather(mine, "batch", axis_index_groups=teams)

    wf = prototypes.astype(jnp.float32)
    proto_n = (wf * lax.rsqrt(jnp.sum(wf * wf, 0, keepdims=True) + eps) * gain[None, :]).astype(
        jnp.bfloat16
    )
    cols = proto_n.shape[1]
    groups = cols // LANES
    count = cols * npr
    rows_all = rows * nb
    expo = jnp.exp(
        jnp.dot(unit_rows(teacher), proto_n, preferred_element_type=jnp.float32) / teacher_temp
    ).astype(jnp.bfloat16)
    expo = lax.optimization_barrier(expo)

    sent = jnp.sum(expo.astype(jnp.float32), 0).reshape(groups, LANES)
    sent = jnp.broadcast_to(sent[None], (nb, groups, LANES))
    for step in range(ITERS):
        last = step + 1 == ITERS
        if step == 1:
            sent, gathered = column_terms(came, expo, nb, gathered)
            gathered = lax.all_gather(gathered, "proto", axis_index_groups=chips)
        elif step:
            sent = column_terms(came, expo, nb)
        came = lax.all_to_all(sent, "batch", 0, 0, tiled=True)
        if not last:
            sent, _ = row_terms(came, expo, npr)
            came = lax.all_to_all(sent, "proto", 0, 0, tiled=True)

    logits = jnp.dot(unit_rows(student), proto_n, preferred_element_type=jnp.float32)
    local_total = jnp.sum(jnp.exp(logits / student_temp), 1)
    team_values = team_products(gathered, proto_n, sent)
    came, team_values, local_total = lax.optimization_barrier((came, team_values, local_total))
    expo_t, student_exp_t, student_t = team_values

    sent, scale_u = row_terms(came, expo, npr, local_total[None])
    came = lax.all_to_all(sent, "proto", 0, 0, tiled=True)
    inverse = 1.0 / jnp.sum(came, 0)
    scale_v = inverse[0]
    by_sender = spread(inverse, "batch", TEAM, teams)

    inv_root = 1.0 / rows_all**0.5
    grad_t = partial_grad(
        expo_t, student_exp_t, student_t, scale_u, by_sender, float(count), inv_root, nb
    )
    parts = lax.all_to_all(grad_t, "batch", 0, 0, tiled=True)
    grad = pl.pallas_call(
        join_kernel,
        out_shape=jax.ShapeDtypeStruct((depth // nb, cols), jnp.float32),
        compiler_params=pltpu.CompilerParams(vmem_limit_bytes=SMALL),
    )(parts)

    scale_u = scale_u.reshape(cols)
    assign = expo.astype(jnp.float32) * scale_u[None, :] * scale_v[:, None]
    targets = (count * assign).astype(jnp.bfloat16)
    return (targets, grad)


def solution(mesh):
    return jax.shard_map(
        local,
        mesh=mesh,
        in_specs=(P("batch", None), P("batch", None), P(None, "proto"), P("proto")),
        out_specs=(P("batch", "proto"), P("batch", "proto")),
        check_vma=False,
    )
```

```python
import functools

import jax
import jax.numpy as jnp
from jax import lax
from jax.experimental import pallas as pl
from jax.experimental.pallas import tpu as pltpu
from jax.sharding import PartitionSpec as P

ITERS = 3
SMALL, PASSING, VMEM = 16 * 2**20, 121 * 2**19, 61 * 2**20
LANES = 128
HELD = 3
TEAM = 8


teacher_temp = 0.04
student_temp = 0.1
eps = 1e-06


def unit_rows(x):
    xf = x.astype(jnp.float32)
    return (xf * lax.rsqrt(jnp.sum(xf * xf, 1, keepdims=True) + eps)).astype(jnp.bfloat16)


def spread(value, axis, size, groups=None):
    sent = jnp.broadcast_to(value[None], (size,) + value.shape)
    return lax.all_to_all(sent, axis, 0, 0, tiled=True, axis_index_groups=groups)


def first_group(groups):
    return jnp.minimum(lax.axis_index("batch") % TEAM * HELD, groups - HELD)


def grad_kernel(count, scale, expo_ref, student_exp_ref, student_ref, u_ref, rows_ref, out_ref, acc, u_wide, diff):
    step = pl.program_id(0)
    rows = rows_ref.shape[2]
    crops = diff.shape[1]

    @pl.when(step == 0)
    def _():
        u = u_ref[pl.ds(first_group(u_ref.shape[0]), HELD), :]
        for g in range(HELD):
            wide = jnp.broadcast_to(u[g : g + 1, :], (LANES, LANES)).T
            u_wide[g * LANES : (g + 1) * LANES, :] = wide

    me = lax.axis_index("batch") % TEAM
    for s in range(crops // rows):
        place = step * (crops // rows) + s
        by = rows_ref[me ^ place ^ ((place >> 1) & 1)]
        for start in range(0, rows, LANES):
            v = by[0:1, start : start + LANES]
            inv_total = by[1:2, start : start + LANES]
            span = slice(s * rows + start, s * rows + start + LANES)
            for g in range(HELD):
                part = slice(g * LANES, (g + 1) * LANES)
                assign = expo_ref[part, span].astype(jnp.float32) * u_wide[part, :] * v
                prob = student_exp_ref[part, span] * inv_total
                diff[part, span] = (count * (prob - assign)).astype(jnp.bfloat16)
    product = jnp.dot(diff[...], student_ref[...], preferred_element_type=jnp.float32)

    @pl.when(step == 0)
    def _():
        acc[...] = product

    @pl.when(step > 0)
    def _():
        acc[...] += product

    @pl.when(step == pl.num_programs(0) - 1)
    def _():
        out_ref[...] = (acc[...].T * scale).reshape(out_ref.shape)


def partial_grad(expo_t, student_exp_t, student, u, by_sender, count, scale, owners):
    part, crops = expo_t.shape
    depth = student.shape[1]
    senders, _, rows = by_sender.shape
    steps = 4
    chunk = crops // steps
    return pl.pallas_call(
        functools.partial(grad_kernel, count, scale),
        grid=(steps,),
        in_specs=[
            pl.BlockSpec((part, chunk), lambda i: (0, i)),
            pl.BlockSpec((part, chunk), lambda i: (0, i)),
            pl.BlockSpec((chunk, depth), lambda i: (i, 0)),
            pl.BlockSpec(u.shape, lambda i: (0, 0)),
            pl.BlockSpec(by_sender.shape, lambda i: (0, 0, 0)),
        ],
        out_specs=pl.BlockSpec((owners, depth // owners, part), lambda i: (0, 0, 0)),
        out_shape=jax.ShapeDtypeStruct((owners, depth // owners, part), jnp.float32),
        scratch_shapes=[
            pltpu.VMEM((part, depth), jnp.float32),
            pltpu.VMEM((part, LANES), jnp.float32),
            pltpu.VMEM((part, chunk), jnp.bfloat16),
        ],
        compiler_params=pltpu.CompilerParams(vmem_limit_bytes=VMEM),
        cost_estimate=pl.CostEstimate(
            flops=2 * part * crops * depth, bytes_accessed=6 * part * crops, transcendentals=0
        ),
    )(expo_t, student_exp_t, student, u, by_sender)


def join_kernel(parts_ref, out_ref):
    teams = parts_ref.shape[0] // TEAM
    groups = out_ref.shape[1] // LANES
    for i in range(TEAM):
        start = min(i * HELD, groups - HELD) * LANES
        total = parts_ref[i]
        for t in range(1, teams):
            total += parts_ref[t * TEAM + i]
        out_ref[:, start : start + HELD * LANES] = total


def row_kernel(came_ref, expo_ref, *refs):
    total_ref, (sent_ref, u_ref) = (refs[0] if len(refs) == 3 else None), refs[-2:]
    u_ref[...] = 1.0 / jnp.sum(came_ref[...], 0)
    rows = expo_ref.shape[0]
    block = 64
    sums = []
    for start in range(0, rows, block):
        acc = jnp.zeros((block, LANES), jnp.float32)
        for j in range(u_ref.shape[0]):
            e = expo_ref[start : start + block, j * LANES : (j + 1) * LANES].astype(jnp.float32)
            acc += e * u_ref[j : j + 1, :]
        sums.append(acc)
    r = jnp.sum(jnp.concatenate(sums, 0).T, 0, keepdims=True)
    peers = sent_ref.shape[0]
    sent_ref[:, 0:1, :] = jnp.broadcast_to(r[None], (peers, 1, rows))
    if total_ref is not None:
        sent_ref[:, 1:2, :] = jnp.broadcast_to(total_ref[...][None], (peers, 1, rows))


def row_terms(came, expo, peers, total=None):
    more = () if total is None else (total,)
    _, groups, _ = came.shape
    rows = expo.shape[0]
    return pl.pallas_call(
        row_kernel,
        out_shape=(
            jax.ShapeDtypeStruct((peers, 1 + len(more), rows), jnp.float32),
            jax.ShapeDtypeStruct((groups, LANES), jnp.float32),
        ),
        compiler_params=pltpu.CompilerParams(vmem_limit_bytes=SMALL),
        cost_estimate=pl.CostEstimate(flops=2 * expo.size, bytes_accessed=2 * expo.size, transcendentals=0),
    )(came, expo, *more)


def column_kernel(came_ref, expo_ref, sent_ref):
    rows = expo_ref.shape[0]
    v = 1.0 / jnp.sum(came_ref[...], 0)
    v = jnp.broadcast_to(v, (LANES, rows)).T
    peers, groups, _ = sent_ref.shape
    for j in range(groups):
        e = expo_ref[:, j * LANES : (j + 1) * LANES].astype(jnp.float32)
        sent_ref[0, j : j + 1, :] = jnp.sum(e * v, 0, keepdims=True)
    sent_ref[1:] = jnp.broadcast_to(sent_ref[0:1], (peers - 1, groups, LANES))


def column_terms(came, expo, peers):
    groups = expo.shape[1] // LANES
    return pl.pallas_call(
        column_kernel,
        out_shape=jax.ShapeDtypeStruct((peers, groups, LANES), jnp.float32),
        compiler_params=pltpu.CompilerParams(vmem_limit_bytes=SMALL),
        cost_estimate=pl.CostEstimate(flops=2 * expo.size, bytes_accessed=2 * expo.size, transcendentals=0),
    )(came, expo)


def after(value, other):
    return pl.pallas_call(
        lambda value_ref, other_ref, out_ref: None,
        in_specs=[pl.BlockSpec(memory_space=pl.ANY)] * 2,
        out_specs=pl.BlockSpec(memory_space=pl.ANY),
        out_shape=jax.ShapeDtypeStruct(value.shape, value.dtype),
        input_output_aliases={0: 0},
        compiler_params=pltpu.CompilerParams(vmem_limit_bytes=VMEM),
    )(value, other)


def team_kernel(own_ref, other_ref, proto_ref, after_ref, expo_ref, student_exp_ref, student_ref, proto_t):
    @pl.when(pl.program_id(0) == 0)
    def _():
        start = pl.multiple_of(first_group(proto_ref.shape[1] // LANES) * LANES, LANES)
        proto_t[...] = proto_ref[:, pl.ds(start, HELD * LANES)].astype(jnp.float32).T.astype(jnp.bfloat16)

    def unit(x):
        return (x * lax.rsqrt(jnp.sum(x * x, 1, keepdims=True) + eps)).astype(jnp.bfloat16)

    across = (((1,), (1,)), ((), ()))
    first = lax.axis_index("proto") % 2 == 0
    proto = proto_t[...]
    t = unit(jnp.where(first, own_ref[0], other_ref[0]))
    s = unit(jnp.where(first, other_ref[0], own_ref[0]))
    student_ref[...] = s
    lt = lax.dot_general(proto, t, across, preferred_element_type=jnp.float32)
    expo_ref[...] = jnp.exp(lt / teacher_temp).astype(jnp.bfloat16)
    ls = lax.dot_general(proto, s, across, preferred_element_type=jnp.float32)
    student_exp_ref[...] = jnp.exp(ls / student_temp)


def team_products(own, other, proto, waited):
    senders, rows, depth = own.shape
    part = HELD * LANES
    return pl.pallas_call(
        team_kernel,
        grid=(senders,),
        in_specs=[
            pl.BlockSpec((1, rows, depth), lambda i: (i, 0, 0)),
            pl.BlockSpec((1, rows, depth), lambda i: (i, 0, 0)),
            pl.BlockSpec(proto.shape, lambda i: (0, 0)),
            pl.BlockSpec(memory_space=pl.ANY),
        ],
        out_specs=[
            pl.BlockSpec((part, rows), lambda i: (0, i)),
            pl.BlockSpec((part, rows), lambda i: (0, i)),
            pl.BlockSpec((rows, depth), lambda i: (i, 0)),
        ],
        out_shape=(
            jax.ShapeDtypeStruct((part, senders * rows), jnp.bfloat16),
            jax.ShapeDtypeStruct((part, senders * rows), jnp.float32),
            jax.ShapeDtypeStruct((senders * rows, depth), jnp.bfloat16),
        ),
        scratch_shapes=[pltpu.VMEM((part, depth), jnp.bfloat16)],
        compiler_params=pltpu.CompilerParams(vmem_limit_bytes=VMEM),
        cost_estimate=pl.CostEstimate(
            flops=4 * part * senders * rows * depth,
            bytes_accessed=10 * 2**20,
            transcendentals=2 * part * senders * rows,
        ),
    )(own, other, proto, waited)


def local(teacher, student, prototypes, gain):
    rows, depth = teacher.shape
    nb, npr = lax.axis_size("batch"), lax.axis_size("proto")
    teams = [[t * TEAM + i for i in range(TEAM)] for t in range(nb // TEAM)]
    core = lax.axis_index("proto") % 2

    mine = jnp.where(core == 0, teacher.astype(jnp.float32), student.astype(jnp.float32))
    held = lax.optimization_barrier(mine)[None]

    def collect(held, flip):
        return lax.ppermute(held, "batch", [(i, i ^ flip) for i in range(nb)])

    wf = prototypes.astype(jnp.float32)
    proto_n = (wf * lax.rsqrt(jnp.sum(wf * wf, 0, keepdims=True) + eps) * gain[None, :]).astype(
        jnp.bfloat16
    )
    cols = proto_n.shape[1]
    groups = cols // LANES
    count = cols * npr
    rows_all = rows * nb
    expo = jnp.exp(
        jnp.dot(unit_rows(teacher), proto_n, preferred_element_type=jnp.float32) / teacher_temp
    ).astype(jnp.bfloat16)
    expo = lax.optimization_barrier(expo)

    sent = jnp.sum(expo.astype(jnp.float32), 0).reshape(groups, LANES)
    sent = jnp.broadcast_to(sent[None], (nb, groups, LANES))
    for step in range(ITERS):
        if step:
            sent = column_terms(came, expo, nb)
        came = lax.all_to_all(sent, "batch", 0, 0, tiled=True)
        if step + 1 < ITERS:
            held = jnp.concatenate([held, collect(held, 1 + 2 * step)])
            sent, _ = row_terms(came, expo, npr)
            held = after(held, sent)
            came = lax.all_to_all(sent, "proto", 0, 0, tiled=True)
    held = jnp.concatenate([held, collect(held, 4)])
    held = after(held, sent)
    other = lax.ppermute(held, "proto", [(i, i ^ 1) for i in range(npr)])

    logits = jnp.dot(unit_rows(student), proto_n, preferred_element_type=jnp.float32)
    local_total = jnp.sum(jnp.exp(logits / student_temp), 1)
    sent, scale_u = row_terms(came, expo, npr, local_total[None])
    came = lax.all_to_all(sent, "proto", 0, 0, tiled=True)
    expo_t, student_exp_t, student_t = team_products(held, other, proto_n, sent)
    inverse = 1.0 / jnp.sum(came, 0)
    scale_v = inverse[0]
    by_sender = spread(inverse, "batch", TEAM, teams)

    inv_root = 1.0 / rows_all**0.5
    grad_t = partial_grad(
        expo_t, student_exp_t, student_t, scale_u, by_sender, float(count), inv_root, nb
    )
    parts = lax.all_to_all(grad_t, "batch", 0, 0, tiled=True)
    grad = pl.pallas_call(
        join_kernel,
        out_shape=jax.ShapeDtypeStruct((depth // nb, cols), jnp.float32),
        compiler_params=pltpu.CompilerParams(vmem_limit_bytes=SMALL),
    )(parts)

    scale_u = scale_u.reshape(cols)
    assign = expo.astype(jnp.float32) * scale_u[None, :] * scale_v[:, None]
    targets = (count * assign).astype(jnp.bfloat16)
    return (targets, grad)


def solution(mesh):
    return jax.shard_map(
        local,
        mesh=mesh,
        in_specs=(P("batch", None), P("batch", None), P(None, "proto"), P("proto")),
        out_specs=(P("batch", "proto"), P("batch", "proto")),
        check_vma=False,
    )
```

```python
import functools

import jax
import jax.numpy as jnp
from jax import lax
from jax.experimental import pallas as pl
from jax.experimental.pallas import tpu as pltpu
from jax.sharding import PartitionSpec as P

ITERS = 3
SMALL, PASSING, VMEM = 16 * 2**20, 121 * 2**19, 61 * 2**20
LANES = 128
HELD = 6
TEAM = 4


teacher_temp = 0.04
student_temp = 0.1
eps = 1e-06


def unit_rows(x):
    xf = x.astype(jnp.float32)
    return (xf * lax.rsqrt(jnp.sum(xf * xf, 1, keepdims=True) + eps)).astype(jnp.bfloat16)


def first_group(groups):
    return jnp.minimum(lax.axis_index("batch") % TEAM * HELD, groups - HELD)


def grad_kernel(count, scale, expo_ref, student_exp_ref, student_ref, u_ref, rows_ref, out_ref, acc, diff):
    step = pl.program_id(0)
    rows = rows_ref.shape[2]
    crops = diff.shape[1]

    me = lax.axis_index("batch") % TEAM
    for s in range(crops // rows):
        place = step * (crops // rows) + s
        by = rows_ref[me ^ place]
        for start in range(0, rows, LANES):
            v = count * by[0:1, start : start + LANES]
            inv_total = count * by[1:2, start : start + LANES]
            span = slice(s * rows + start, s * rows + start + LANES)
            for g in range(HELD):
                part = slice(g * LANES, (g + 1) * LANES)
                assign = expo_ref[part, span].astype(jnp.float32) * u_ref[part, :] * v
                prob = student_exp_ref[part, span] * inv_total
                diff[part, span] = (prob - assign).astype(jnp.bfloat16)
    product = jnp.dot(diff[...], student_ref[...], preferred_element_type=jnp.float32)

    @pl.when(step == 0)
    def _():
        acc[...] = product

    @pl.when(step > 0)
    def _():
        acc[...] += product

    @pl.when(step == pl.num_programs(0) - 1)
    def _():
        out_ref[...] = (acc[...].T * scale).reshape(out_ref.shape)


def partial_grad(expo_t, student_exp_t, student, u, by_sender, count, scale, owners):
    part, crops = expo_t.shape
    depth = student.shape[1]
    senders, _, rows = by_sender.shape
    steps = 4
    chunk = crops // steps
    return pl.pallas_call(
        functools.partial(grad_kernel, count, scale),
        grid=(steps,),
        in_specs=[
            pl.BlockSpec((part, chunk), lambda i: (0, i)),
            pl.BlockSpec((part, chunk), lambda i: (0, i)),
            pl.BlockSpec((chunk, depth), lambda i: (i, 0)),
            pl.BlockSpec(u.shape, lambda i: (0, 0)),
            pl.BlockSpec(by_sender.shape, lambda i: (0, 0, 0)),
        ],
        out_specs=pl.BlockSpec((owners, depth // owners, part), lambda i: (0, 0, 0)),
        out_shape=jax.ShapeDtypeStruct((owners, depth // owners, part), jnp.float32),
        scratch_shapes=[
            pltpu.VMEM((part, depth), jnp.float32),
            pltpu.VMEM((part, chunk), jnp.bfloat16),
        ],
        compiler_params=pltpu.CompilerParams(vmem_limit_bytes=VMEM),
        cost_estimate=pl.CostEstimate(
            flops=2 * part * crops * depth, bytes_accessed=6 * part * crops, transcendentals=0
        ),
    )(expo_t, student_exp_t, student, u, by_sender)


def join_kernel(parts_ref, out_ref):
    teams = parts_ref.shape[0] // TEAM
    groups = out_ref.shape[1] // LANES
    for i in range(TEAM):
        start = min(i * HELD, groups - HELD) * LANES
        total = parts_ref[i]
        for t in range(1, teams):
            total += parts_ref[t * TEAM + i]
        out_ref[:, start : start + HELD * LANES] = total


def start_kernel(teacher_ref, student_ref, proto_ref, gain_ref, mine_ref, proto_n_ref, expo_ref, sent_ref):
    t = teacher_ref[...].astype(jnp.float32)
    first = lax.axis_index("proto") % 2 == 0
    mine_ref[0] = jnp.where(first, t, student_ref[...].astype(jnp.float32))
    t = (t * lax.rsqrt(jnp.sum(t * t, 1, keepdims=True) + eps)).astype(jnp.bfloat16)
    peers, groups, _ = sent_ref.shape
    for j in range(0, groups, 2):
        span = slice(j * LANES, (j + 2) * LANES)
        w = proto_ref[:, span].astype(jnp.float32)
        gains = jnp.concatenate([gain_ref[j : j + 1, :], gain_ref[j + 1 : j + 2, :]], 1)
        w = (w * lax.rsqrt(jnp.sum(w * w, 0, keepdims=True) + eps) * gains).astype(jnp.bfloat16)
        proto_n_ref[:, span] = w
        e = jnp.exp(jnp.dot(t, w, preferred_element_type=jnp.float32) / teacher_temp)
        e = e.astype(jnp.bfloat16)
        expo_ref[:, span] = e
        c = jnp.sum(e.astype(jnp.float32), 0, keepdims=True)
        sent_ref[0, j : j + 1, :] = c[:, :LANES]
        sent_ref[0, j + 1 : j + 2, :] = c[:, LANES:]
    sent_ref[1:] = jnp.broadcast_to(sent_ref[0:1], (peers - 1, groups, LANES))


def start(teacher, student, prototypes, gain, peers):
    rows, depth = teacher.shape
    cols = prototypes.shape[1]
    groups = cols // LANES
    return pl.pallas_call(
        start_kernel,
        out_shape=(
            jax.ShapeDtypeStruct((1, rows, depth), jnp.float32),
            jax.ShapeDtypeStruct((depth, cols), jnp.bfloat16),
            jax.ShapeDtypeStruct((rows, cols), jnp.bfloat16),
            jax.ShapeDtypeStruct((peers, groups, LANES), jnp.float32),
        ),
        compiler_params=pltpu.CompilerParams(vmem_limit_bytes=VMEM),
        cost_estimate=pl.CostEstimate(
            flops=2 * rows * depth * cols, bytes_accessed=6 * depth * cols, transcendentals=rows * cols
        ),
    )(teacher, student, prototypes, gain.reshape(groups, LANES))


def local_call(kernel, operands, waited, out_shape, flops):
    n = len(operands)

    def body(*refs):
        kernel(*refs[:n], *refs[n + len(waited) :])

    return pl.pallas_call(
        body,
        in_specs=[pl.BlockSpec()] * n + [pl.BlockSpec(memory_space=pl.ANY)] * len(waited),
        out_shape=out_shape,
        compiler_params=pltpu.CompilerParams(vmem_limit_bytes=SMALL),
        cost_estimate=pl.CostEstimate(flops=flops, bytes_accessed=flops, transcendentals=0),
    )(*operands, *waited)


def row_kernel(came_ref, expo_ref, *refs):
    total_ref, (sent_ref, u_ref) = (refs[0] if len(refs) == 3 else None), refs[-2:]
    u_ref[...] = 1.0 / jnp.sum(came_ref[...], 0)
    rows = expo_ref.shape[0]
    block = 64
    sums = []
    for first in range(0, rows, block):
        acc = jnp.zeros((block, LANES), jnp.float32)
        for j in range(u_ref.shape[0]):
            e = expo_ref[first : first + block, j * LANES : (j + 1) * LANES].astype(jnp.float32)
            acc += e * u_ref[j : j + 1, :]
        sums.append(acc)
    r = jnp.sum(jnp.concatenate(sums, 0).T, 0, keepdims=True)
    peers = sent_ref.shape[0]
    sent_ref[:, 0:1, :] = jnp.broadcast_to(r[None], (peers, 1, rows))
    if total_ref is not None:
        sent_ref[:, 1:2, :] = jnp.broadcast_to(total_ref[...][None], (peers, 1, rows))


def row_terms(came, expo, peers, *waited, total=None):
    more = () if total is None else (total,)
    rows = expo.shape[0]
    out_shape = (
        jax.ShapeDtypeStruct((peers, 1 + len(more), rows), jnp.float32),
        jax.ShapeDtypeStruct(came.shape[1:], jnp.float32),
    )
    return local_call(row_kernel, (came, expo, *more), waited, out_shape, 2 * expo.size)


def column_kernel(came_ref, expo_ref, sent_ref):
    rows = expo_ref.shape[0]
    v = 1.0 / jnp.sum(came_ref[...], 0)
    v = jnp.broadcast_to(v, (LANES, rows)).T
    peers, groups, _ = sent_ref.shape
    for j in range(groups):
        e = expo_ref[:, j * LANES : (j + 1) * LANES].astype(jnp.float32)
        sent_ref[0, j : j + 1, :] = jnp.sum(e * v, 0, keepdims=True)
    sent_ref[1:] = jnp.broadcast_to(sent_ref[0:1], (peers - 1, groups, LANES))


def column_terms(came, expo, peers, *waited):
    out_shape = jax.ShapeDtypeStruct((peers, expo.shape[1] // LANES, LANES), jnp.float32)
    return local_call(column_kernel, (came, expo), waited, out_shape, 2 * expo.size)


def team_rows_kernel(came_ref, sent_ref, own_ref):
    own_ref[...] = 1.0 / jnp.sum(came_ref[...], 0)
    sent_ref[...] = jnp.broadcast_to(own_ref[...][None], sent_ref.shape)


def team_rows(came, *waited):
    out_shape = (
        jax.ShapeDtypeStruct((TEAM,) + came.shape[1:], jnp.float32),
        jax.ShapeDtypeStruct(came.shape[1:], jnp.float32),
    )
    return local_call(team_rows_kernel, (came,), waited, out_shape, came.size)


def after(value, other):
    return pl.pallas_call(
        lambda value_ref, other_ref, out_ref: None,
        in_specs=[pl.BlockSpec(memory_space=pl.ANY)] * 2,
        out_specs=pl.BlockSpec(memory_space=pl.ANY),
        out_shape=jax.ShapeDtypeStruct(value.shape, value.dtype),
        input_output_aliases={0: 0},
        compiler_params=pltpu.CompilerParams(vmem_limit_bytes=VMEM),
    )(value, other)


def team_kernel(own_ref, other_ref, proto_ref, u_ref, after_ref, expo_ref, student_exp_ref, student_ref, u_wide_ref, done_ref, proto_t):
    @pl.when(pl.program_id(0) == 0)
    def _():
        start = pl.multiple_of(first_group(proto_ref.shape[1] // LANES) * LANES, LANES)
        proto_t[...] = proto_ref[:, pl.ds(start, HELD * LANES)].astype(jnp.float32).T.astype(jnp.bfloat16)
        u = u_ref[pl.ds(first_group(u_ref.shape[0]), HELD), :]
        for g in range(HELD):
            wide = jnp.broadcast_to(u[g : g + 1, :], (LANES, LANES)).T
            u_wide_ref[g * LANES : (g + 1) * LANES, :] = wide
        done_ref[...] = jnp.zeros_like(done_ref)

    def unit(x):
        return (x * lax.rsqrt(jnp.sum(x * x, 1, keepdims=True) + eps)).astype(jnp.bfloat16)

    across = (((1,), (1,)), ((), ()))
    first = lax.axis_index("proto") % 2 == 0
    proto = proto_t[...]
    t = unit(jnp.where(first, own_ref[0], other_ref[0]))
    s = unit(jnp.where(first, other_ref[0], own_ref[0]))
    student_ref[...] = s
    lt = lax.dot_general(proto, t, across, preferred_element_type=jnp.float32)
    expo_ref[...] = jnp.exp(lt / teacher_temp).astype(jnp.bfloat16)
    ls = lax.dot_general(proto, s, across, preferred_element_type=jnp.float32)
    student_exp_ref[...] = jnp.exp(ls / student_temp)


def team_products(own, other, proto, u, waited):
    senders, rows, depth = own.shape
    part = HELD * LANES
    return pl.pallas_call(
        team_kernel,
        grid=(senders,),
        in_specs=[
            pl.BlockSpec((1, rows, depth), lambda i: (i, 0, 0)),
            pl.BlockSpec((1, rows, depth), lambda i: (i, 0, 0)),
            pl.BlockSpec(proto.shape, lambda i: (0, 0)),
            pl.BlockSpec(u.shape, lambda i: (0, 0)),
            pl.BlockSpec(memory_space=pl.ANY),
        ],
        out_specs=[
            pl.BlockSpec((part, rows), lambda i: (0, i)),
            pl.BlockSpec((part, rows), lambda i: (0, i)),
            pl.BlockSpec((rows, depth), lambda i: (i, 0)),
            pl.BlockSpec((part, LANES), lambda i: (0, 0)),
            pl.BlockSpec((8, LANES), lambda i: (0, 0)),
        ],
        out_shape=(
            jax.ShapeDtypeStruct((part, senders * rows), jnp.bfloat16),
            jax.ShapeDtypeStruct((part, senders * rows), jnp.float32),
            jax.ShapeDtypeStruct((senders * rows, depth), jnp.bfloat16),
            jax.ShapeDtypeStruct((part, LANES), jnp.float32),
            jax.ShapeDtypeStruct((8, LANES), jnp.float32),
        ),
        scratch_shapes=[pltpu.VMEM((part, depth), jnp.bfloat16)],
        compiler_params=pltpu.CompilerParams(vmem_limit_bytes=VMEM),
        cost_estimate=pl.CostEstimate(
            flops=4 * part * senders * rows * depth,
            bytes_accessed=10 * 2**20,
            transcendentals=2 * part * senders * rows,
        ),
    )(own, other, proto, u, waited)


def local(teacher, student, prototypes, gain):
    rows, depth = teacher.shape
    nb, npr = lax.axis_size("batch"), lax.axis_size("proto")
    teams = [[t * TEAM + i for i in range(TEAM)] for t in range(nb // TEAM)]
    cols = prototypes.shape[1]
    count = cols * npr
    rows_all = rows * nb

    mine, proto_n, expo, sent = start(teacher, student, prototypes, gain, nb)

    def member(rows, flip):
        return lax.ppermute(rows, "batch", [(i, i ^ flip) for i in range(nb)])

    held = [mine, member(mine, 1), None, member(mine, 3)]
    came = lax.all_to_all(sent, "batch", 0, 0, tiled=True)
    sent, _ = row_terms(came, expo, npr, held[1], held[3])
    came = lax.all_to_all(sent, "proto", 0, 0, tiled=True)
    sent = column_terms(came, expo, nb)
    held[2] = member(after(mine, sent), 2)
    came = lax.all_to_all(sent, "batch", 0, 0, tiled=True)
    sent, _ = row_terms(came, expo, npr, held[2])
    own = jnp.concatenate(held)
    came = lax.all_to_all(sent, "proto", 0, 0, tiled=True)
    sent = column_terms(came, expo, nb)
    other = lax.ppermute(own, "proto", [(i, i ^ 1) for i in range(npr)])
    came = lax.all_to_all(sent, "batch", 0, 0, tiled=True)

    logits = jnp.dot(unit_rows(student), proto_n, preferred_element_type=jnp.float32)
    local_total = jnp.sum(jnp.exp(logits / student_temp), 1)
    sent, scale_u = row_terms(came, expo, npr, other, total=local_total[None])
    came = lax.all_to_all(sent, "proto", 0, 0, tiled=True)
    *team_values, done = team_products(own, other, proto_n, scale_u, sent)
    sent, inverse = team_rows(came, done)
    scale_v = inverse[0]
    by_sender = lax.all_to_all(sent, "batch", 0, 0, tiled=True, axis_index_groups=teams)

    inv_root = 1.0 / rows_all**0.5
    grad_t = partial_grad(*team_values, by_sender, float(count), inv_root, nb)
    parts = lax.all_to_all(grad_t, "batch", 0, 0, tiled=True)
    grad = pl.pallas_call(
        join_kernel,
        out_shape=jax.ShapeDtypeStruct((depth // nb, cols), jnp.float32),
        compiler_params=pltpu.CompilerParams(vmem_limit_bytes=SMALL),
    )(parts)

    scale_u = scale_u.reshape(cols)
    assign = expo.astype(jnp.float32) * scale_u[None, :] * scale_v[:, None]
    targets = (count * assign).astype(jnp.bfloat16)
    return (targets, grad)


def solution(mesh):
    return jax.shard_map(
        local,
        mesh=mesh,
        in_specs=(P("batch", None), P("batch", None), P(None, "proto"), P("proto")),
        out_specs=(P("batch", "proto"), P("batch", "proto")),
        check_vma=False,
    )
```

```python
import functools

import jax
import jax.numpy as jnp
from jax import lax
from jax.experimental import pallas as pl
from jax.experimental.pallas import tpu as pltpu
from jax.sharding import PartitionSpec as P

ITERS = 3
SMALL, VMEM = 16 * 2**20, 61 * 2**20
TEAM_VMEM, GRAD_VMEM = 56 * 2**20, 61 * 2**20
LANES = 128
HELD = 6
SPLIT = 4
HALVES = 2
TEAM = 4


teacher_temp = 0.04
student_temp = 0.1
eps = 1e-06


def unit_rows(x):
    xf = x.astype(jnp.float32)
    return (xf * lax.rsqrt(jnp.sum(xf * xf, 1, keepdims=True) + eps)).astype(jnp.bfloat16)


def first_group(groups):
    return jnp.minimum(lax.axis_index("batch") % TEAM * HELD, groups - HELD)


def grad_kernel(count, scale, *refs):
    exps, student_exps = refs[:SPLIT], refs[SPLIT : 2 * SPLIT]
    student_ref, u_ref, rows_ref, out_ref, diff = refs[2 * SPLIT :]
    rows = rows_ref.shape[2]
    chunk = diff.shape[0]
    piece = chunk // SPLIT
    me = lax.axis_index("batch") % TEAM
    u = u_ref[pl.ds(first_group(u_ref.shape[0]) + pl.program_id(0) * (chunk // LANES), chunk // LANES), :]
    wide = [jnp.broadcast_to(u[g : g + 1, :], (LANES, LANES)).T for g in range(chunk // LANES)]
    wide = jnp.concatenate(wide, 0)
    for place in range(TEAM):
        by = rows_ref[me ^ place] * count
        for first in range(0, rows, LANES):
            v = by[0:1, first : first + LANES]
            inv_total = by[1:2, first : first + LANES]
            span = slice(place * rows + first, place * rows + first + LANES)
            for i in range(SPLIT):
                part = slice(i * piece, (i + 1) * piece)
                assign = exps[i][:, span].astype(jnp.float32) * wide[part, :] * v
                prob = student_exps[i][:, span] * inv_total
                diff[part, span] = (prob - assign).astype(jnp.bfloat16)
    product = jnp.dot(diff[...], student_ref[...], preferred_element_type=jnp.float32)
    out_ref[...] = (product.T * scale).reshape(out_ref.shape)


def partial_grad(expo_t, student_exp_t, student, u, by_sender, count, scale, owners):
    part, crops = expo_t.shape
    depth = student.shape[1]
    steps = 2
    chunk = part // steps
    piece = chunk // SPLIT

    def pieces():
        return [pl.BlockSpec((piece, crops), lambda i, k=k: (i * SPLIT + k, 0)) for k in range(SPLIT)]

    return pl.pallas_call(
        functools.partial(grad_kernel, count, scale),
        grid=(steps,),
        in_specs=[
            *pieces(),
            *pieces(),
            pl.BlockSpec(student.shape, lambda i: (0, 0)),
            pl.BlockSpec(u.shape, lambda i: (0, 0)),
            pl.BlockSpec(by_sender.shape, lambda i: (0, 0, 0)),
        ],
        out_specs=pl.BlockSpec((owners, depth // owners, chunk), lambda i: (0, 0, i)),
        out_shape=jax.ShapeDtypeStruct((owners, depth // owners, part), jnp.float32),
        scratch_shapes=[pltpu.VMEM((chunk, crops), jnp.bfloat16)],
        compiler_params=pltpu.CompilerParams(vmem_limit_bytes=GRAD_VMEM),
        cost_estimate=pl.CostEstimate(
            flops=2 * part * crops * depth, bytes_accessed=6 * part * crops, transcendentals=0
        ),
    )(*[expo_t] * SPLIT, *[student_exp_t] * SPLIT, student, u, by_sender)


def join_kernel(parts_ref, out_ref):
    teams = parts_ref.shape[0] // TEAM
    groups = out_ref.shape[1] // LANES
    for i in range(TEAM):
        start = min(i * HELD, groups - HELD) * LANES
        total = parts_ref[i]
        for t in range(1, teams):
            total += parts_ref[t * TEAM + i]
        out_ref[:, start : start + HELD * LANES] = total


def start_kernel(teacher_ref, student_ref, proto_ref, gain_ref, mine_ref, proto_n_ref, expo_ref, sent_ref, unit, terms):
    step = pl.program_id(0)
    here = proto_ref.shape[1] // LANES

    @pl.when(step == 0)
    def _():
        t = teacher_ref[...].astype(jnp.float32)
        first = lax.axis_index("proto") % 2 == 0
        mine_ref[0] = jnp.where(first, t, student_ref[...].astype(jnp.float32))
        unit[...] = (t * lax.rsqrt(jnp.sum(t * t, 1, keepdims=True) + eps)).astype(jnp.bfloat16)

    for j in range(here):
        span = slice(j * LANES, (j + 1) * LANES)
        w = proto_ref[:, span].astype(jnp.float32)
        gains = gain_ref[pl.ds(step * here + j, 1), :]
        w = (w * lax.rsqrt(jnp.sum(w * w, 0, keepdims=True) + eps) * gains).astype(jnp.bfloat16)
        proto_n_ref[:, span] = w
    e = jnp.exp(jnp.dot(unit[...], proto_n_ref[...], preferred_element_type=jnp.float32) / teacher_temp)
    e = e.astype(jnp.bfloat16)
    cols = proto_ref.shape[1]
    expo_ref[:, pl.ds(pl.multiple_of(step * cols, LANES), cols)] = e
    c = jnp.sum(e.astype(jnp.float32), 0, keepdims=True)
    terms[pl.ds(step, 1), :] = c

    @pl.when(step == pl.num_programs(0) - 1)
    def _():
        sent_ref[...] = jnp.broadcast_to(terms[...][None], sent_ref.shape)


def start(teacher, student, prototypes, gain, peers):
    rows, depth = teacher.shape
    cols = prototypes.shape[1]
    groups = cols // LANES
    steps = HALVES
    chunk = cols // steps
    return pl.pallas_call(
        start_kernel,
        grid=(steps,),
        in_specs=[
            pl.BlockSpec((rows, depth), lambda i: (0, 0)),
            pl.BlockSpec((rows, depth), lambda i: (0, 0)),
            pl.BlockSpec((depth, chunk), lambda i: (0, i)),
            pl.BlockSpec((groups, LANES), lambda i: (0, 0)),
        ],
        out_specs=[
            pl.BlockSpec((1, rows, depth), lambda i: (0, 0, 0)),
            pl.BlockSpec((depth, chunk), lambda i: (0, i)),
            pl.BlockSpec(memory_space=pltpu.VMEM),
            pl.BlockSpec(memory_space=pltpu.VMEM),
        ],
        out_shape=(
            jax.ShapeDtypeStruct((1, rows, depth), jnp.float32),
            jax.ShapeDtypeStruct((depth, cols), jnp.bfloat16),
            pltpu.VMEM((rows, cols), jnp.bfloat16),
            pltpu.VMEM((peers, steps, chunk), jnp.float32),
        ),
        scratch_shapes=[pltpu.VMEM((rows, depth), jnp.bfloat16), pltpu.VMEM((steps, chunk), jnp.float32)],
        compiler_params=pltpu.CompilerParams(vmem_limit_bytes=60 * 2**20),
        cost_estimate=pl.CostEstimate(
            flops=2 * rows * depth * cols, bytes_accessed=6 * depth * cols, transcendentals=rows * cols
        ),
    )(teacher, student, prototypes, gain.reshape(groups, LANES))


def local_call(kernel, operands, waited, out_shape, flops):
    n = len(operands)

    def body(*refs):
        kernel(*refs[:n], *refs[n + len(waited) :])

    return pl.pallas_call(
        body,
        in_specs=[pl.BlockSpec()] * n + [pl.BlockSpec(memory_space=pl.ANY)] * len(waited),
        out_shape=out_shape,
        compiler_params=pltpu.CompilerParams(vmem_limit_bytes=SMALL),
        cost_estimate=pl.CostEstimate(flops=flops, bytes_accessed=flops, transcendentals=0),
    )(*operands, *waited)


def row_kernel(came_ref, expo_ref, *refs):
    total_ref, (sent_ref, u_ref) = (refs[0] if len(refs) == 3 else None), refs[-2:]
    u = 1.0 / jnp.sum(came_ref[...], 0)
    half = u.shape[1] // LANES
    for j in range(u_ref.shape[0]):
        u_ref[j : j + 1, :] = u[j // half : j // half + 1, j % half * LANES : (j % half + 1) * LANES]
    rows = expo_ref.shape[0]
    block = 64
    sums = []
    for first in range(0, rows, block):
        acc = jnp.zeros((block, LANES), jnp.float32)
        for j in range(u_ref.shape[0]):
            e = expo_ref[first : first + block, j * LANES : (j + 1) * LANES].astype(jnp.float32)
            acc += e * u_ref[j : j + 1, :]
        sums.append(acc)
    r = jnp.sum(jnp.concatenate(sums, 0).T, 0, keepdims=True)
    peers = sent_ref.shape[0]
    sent_ref[:, 0:1, :] = jnp.broadcast_to(r[None], (peers, 1, rows))
    if total_ref is not None:
        sent_ref[:, 1:2, :] = jnp.broadcast_to(total_ref[...][None], (peers, 1, rows))


def row_terms(came, expo, peers, *waited, total=None):
    more = () if total is None else (total,)
    rows = expo.shape[0]
    out_shape = (
        jax.ShapeDtypeStruct((peers, 1 + len(more), rows), jnp.float32),
        jax.ShapeDtypeStruct((expo.shape[1] // LANES, LANES), jnp.float32),
    )
    return local_call(row_kernel, (came, expo, *more), waited, out_shape, 2 * expo.size)


def column_kernel(came_ref, expo_ref, sent_ref):
    rows = expo_ref.shape[0]
    v = 1.0 / jnp.sum(came_ref[...], 0)
    v = jnp.broadcast_to(v, (LANES, rows)).T
    peers, halves, cols = sent_ref.shape
    for h in range(halves):
        for first in range(0, cols, LANES):
            e = expo_ref[:, h * cols + first : h * cols + first + LANES].astype(jnp.float32)
            sent_ref[0, h : h + 1, first : first + LANES] = jnp.sum(e * v, 0, keepdims=True)
    sent_ref[1:] = jnp.broadcast_to(sent_ref[0:1], (peers - 1, halves, cols))


def column_terms(came, expo, peers, *waited):
    out_shape = jax.ShapeDtypeStruct((peers, HALVES, expo.shape[1] // HALVES), jnp.float32)
    return local_call(column_kernel, (came, expo), waited, out_shape, 2 * expo.size)


def team_rows_kernel(came_ref, sent_ref, own_ref):
    own_ref[...] = 1.0 / jnp.sum(came_ref[...], 0)
    sent_ref[...] = jnp.broadcast_to(own_ref[...][None], sent_ref.shape)


def team_rows(came, *waited):
    out_shape = (
        jax.ShapeDtypeStruct((TEAM,) + came.shape[1:], jnp.float32),
        jax.ShapeDtypeStruct(came.shape[1:], jnp.float32),
    )
    return local_call(team_rows_kernel, (came,), waited, out_shape, came.size)


def team_kernel(own_ref, other_ref, proto_ref, after_ref, expo_ref, student_exp_ref, student_ref, done_ref, proto_t):
    @pl.when(pl.program_id(0) == 0)
    def _():
        start = pl.multiple_of(first_group(proto_ref.shape[1] // LANES) * LANES, LANES)
        proto_t[...] = proto_ref[:, pl.ds(start, HELD * LANES)].astype(jnp.float32).T.astype(jnp.bfloat16)
        done_ref[...] = jnp.zeros_like(done_ref)

    def unit(x):
        return (x * lax.rsqrt(jnp.sum(x * x, 1, keepdims=True) + eps)).astype(jnp.bfloat16)

    across = (((1,), (1,)), ((), ()))
    first = lax.axis_index("proto") % 2 == 0
    proto = proto_t[...]
    t = unit(jnp.where(first, own_ref[0], other_ref[0]))
    s = unit(jnp.where(first, other_ref[0], own_ref[0]))
    student_ref[...] = s
    lt = lax.dot_general(proto, t, across, preferred_element_type=jnp.float32)
    expo_ref[...] = jnp.exp(lt / teacher_temp).astype(jnp.bfloat16)
    ls = lax.dot_general(proto, s, across, preferred_element_type=jnp.float32)
    student_exp_ref[...] = jnp.exp(ls / student_temp)


def team_products(own, other, proto, waited):
    senders, rows, depth = own.shape
    part = HELD * LANES
    return pl.pallas_call(
        team_kernel,
        grid=(senders,),
        in_specs=[
            pl.BlockSpec((1, rows, depth), lambda i: (i, 0, 0)),
            pl.BlockSpec((1, rows, depth), lambda i: (i, 0, 0)),
            pl.BlockSpec(proto.shape, lambda i: (0, 0)),
            pl.BlockSpec(memory_space=pl.ANY),
        ],
        out_specs=[
            pl.BlockSpec((part, rows), lambda i: (0, i)),
            pl.BlockSpec((part, rows), lambda i: (0, i)),
            pl.BlockSpec((rows, depth), lambda i: (i, 0)),
            pl.BlockSpec((8, LANES), lambda i: (0, 0)),
        ],
        out_shape=(
            jax.ShapeDtypeStruct((part, senders * rows), jnp.bfloat16),
            jax.ShapeDtypeStruct((part, senders * rows), jnp.float32),
            jax.ShapeDtypeStruct((senders * rows, depth), jnp.bfloat16),
            jax.ShapeDtypeStruct((8, LANES), jnp.float32),
        ),
        scratch_shapes=[pltpu.VMEM((part, depth), jnp.bfloat16)],
        compiler_params=pltpu.CompilerParams(vmem_limit_bytes=TEAM_VMEM),
        cost_estimate=pl.CostEstimate(
            flops=4 * part * senders * rows * depth,
            bytes_accessed=10 * 2**20,
            transcendentals=2 * part * senders * rows,
        ),
    )(own, other, proto, waited)


def local(teacher, student, prototypes, gain):
    rows, depth = teacher.shape
    nb, npr = lax.axis_size("batch"), lax.axis_size("proto")
    teams = [[t * TEAM + i for i in range(TEAM)] for t in range(nb // TEAM)]
    cols = prototypes.shape[1]
    count = cols * npr
    rows_all = rows * nb

    mine, proto_n, expo, sent = start(teacher, student, prototypes, gain, nb)

    def member(rows, flip):
        return lax.ppermute(rows, "batch", [(i, i ^ flip) for i in range(nb)])

    held = [mine, member(mine, 1), None, member(mine, 3)]
    came = lax.all_to_all(sent, "batch", 0, 0, tiled=True)
    sent, _ = row_terms(came, expo, npr, held[1], held[3])
    came = lax.all_to_all(sent, "proto", 0, 0, tiled=True)
    sent = column_terms(came, expo, nb)
    held[2] = member(mine, 2)
    came = lax.all_to_all(sent, "batch", 0, 0, tiled=True)
    sent, _ = row_terms(came, expo, npr, held[2])
    own = jnp.concatenate(held)
    came = lax.all_to_all(sent, "proto", 0, 0, tiled=True)
    sent = column_terms(came, expo, nb)
    other = lax.ppermute(own, "proto", [(i, i ^ 1) for i in range(npr)])
    came = lax.all_to_all(sent, "batch", 0, 0, tiled=True)

    logits = jnp.dot(unit_rows(student), proto_n, preferred_element_type=jnp.float32)
    local_total = jnp.sum(jnp.exp(logits / student_temp), 1)
    sent, scale_u = row_terms(came, expo, npr, other, total=local_total[None])
    came = lax.all_to_all(sent, "proto", 0, 0, tiled=True)
    *team_values, done = team_products(own, other, proto_n, sent)
    sent, inverse = team_rows(came, done)
    scale_v = inverse[0]
    by_sender = lax.all_to_all(sent, "batch", 0, 0, tiled=True, axis_index_groups=teams)

    inv_root = 1.0 / rows_all**0.5
    grad_t = partial_grad(*team_values, scale_u, by_sender, float(count), inv_root, nb)
    parts = lax.all_to_all(grad_t, "batch", 0, 0, tiled=True)
    grad = pl.pallas_call(
        join_kernel,
        out_shape=jax.ShapeDtypeStruct((depth // nb, cols), jnp.float32),
        compiler_params=pltpu.CompilerParams(vmem_limit_bytes=SMALL),
    )(parts)

    scale_u = scale_u.reshape(cols)
    assign = expo.astype(jnp.float32) * scale_u[None, :] * scale_v[:, None]
    targets = (count * assign).astype(jnp.bfloat16)
    return (targets, grad)


def solution(mesh):
    return jax.shard_map(
        local,
        mesh=mesh,
        in_specs=(P("batch", None), P("batch", None), P(None, "proto"), P("proto")),
        out_specs=(P("batch", "proto"), P("batch", "proto")),
        check_vma=False,
    )
```

```python
import functools

import jax
import jax.numpy as jnp
from jax import lax
from jax.experimental import pallas as pl
from jax.experimental.pallas import tpu as pltpu
from jax.sharding import PartitionSpec as P

ITERS = 3
SMALL, VMEM = 16 * 2**20, 61 * 2**20
TEAM_VMEM, GRAD_VMEM = 56 * 2**20, 61 * 2**20
LANES = 128
HELD = 6
SPLIT = 4
HALVES = 2
TEAM = 4


teacher_temp = 0.04
student_temp = 0.1
eps = 1e-06


def unit_rows(x):
    xf = x.astype(jnp.float32)
    return (xf * lax.rsqrt(jnp.sum(xf * xf, 1, keepdims=True) + eps)).astype(jnp.bfloat16)


def first_group(groups):
    return jnp.minimum(lax.axis_index("batch") % TEAM * HELD, groups - HELD)


def grad_kernel(count, scale, *refs):
    exps, student_exps = refs[:SPLIT], refs[SPLIT : 2 * SPLIT]
    student_ref, u_ref, came_ref, out_ref, own_ref, diff = refs[2 * SPLIT :]
    senders = came_ref.shape[0] // TEAM
    rows = came_ref.shape[2]
    chunk = diff.shape[0]
    piece = chunk // SPLIT
    me = lax.axis_index("batch") % TEAM
    u = u_ref[pl.ds(first_group(u_ref.shape[0]) + pl.program_id(0) * (chunk // LANES), chunk // LANES), :]
    wide = [jnp.broadcast_to(u[g : g + 1, :], (LANES, LANES)).T for g in range(chunk // LANES)]
    wide = jnp.concatenate(wide, 0)
    for place in range(TEAM):
        by = 1.0 / jnp.sum(came_ref[pl.ds((me ^ place) * senders, senders)], 0)
        if place == 0:
            own_ref[...] = by
        by = by * count
        for first in range(0, rows, LANES):
            v = by[0:1, first : first + LANES]
            inv_total = by[1:2, first : first + LANES]
            span = slice(place * rows + first, place * rows + first + LANES)
            for i in range(SPLIT):
                part = slice(i * piece, (i + 1) * piece)
                assign = exps[i][:, span].astype(jnp.float32) * wide[part, :] * v
                prob = student_exps[i][:, span] * inv_total
                diff[part, span] = (prob - assign).astype(jnp.bfloat16)
    product = jnp.dot(diff[...], student_ref[...], preferred_element_type=jnp.float32)
    out_ref[...] = (product.T * scale).reshape(out_ref.shape)


def partial_grad(expo_t, student_exp_t, student, u, came, count, scale, owners):
    part, crops = expo_t.shape
    depth = student.shape[1]
    steps = 2
    chunk = part // steps
    piece = chunk // SPLIT

    def pieces():
        return [pl.BlockSpec((piece, crops), lambda i, k=k: (i * SPLIT + k, 0)) for k in range(SPLIT)]

    return pl.pallas_call(
        functools.partial(grad_kernel, count, scale),
        grid=(steps,),
        in_specs=[
            *pieces(),
            *pieces(),
            pl.BlockSpec(student.shape, lambda i: (0, 0)),
            pl.BlockSpec(u.shape, lambda i: (0, 0)),
            pl.BlockSpec(came.shape, lambda i: (0, 0, 0)),
        ],
        out_specs=[
            pl.BlockSpec((owners, depth // owners, chunk), lambda i: (0, 0, i)),
            pl.BlockSpec(came.shape[1:], lambda i: (0, 0)),
        ],
        out_shape=(
            jax.ShapeDtypeStruct((owners, depth // owners, part), jnp.float32),
            jax.ShapeDtypeStruct(came.shape[1:], jnp.float32),
        ),
        scratch_shapes=[pltpu.VMEM((chunk, crops), jnp.bfloat16)],
        compiler_params=pltpu.CompilerParams(vmem_limit_bytes=GRAD_VMEM),
        cost_estimate=pl.CostEstimate(
            flops=2 * part * crops * depth, bytes_accessed=6 * part * crops, transcendentals=0
        ),
    )(*[expo_t] * SPLIT, *[student_exp_t] * SPLIT, student, u, came)


def join_kernel(parts_ref, out_ref):
    teams = parts_ref.shape[0] // TEAM
    groups = out_ref.shape[1] // LANES
    for i in range(TEAM):
        start = min(i * HELD, groups - HELD) * LANES
        total = parts_ref[i]
        for t in range(1, teams):
            total += parts_ref[t * TEAM + i]
        out_ref[:, start : start + HELD * LANES] = total


def start_kernel(teacher_ref, student_ref, proto_ref, gain_ref, mine_ref, proto_n_ref, expo_ref, sent_ref, unit, terms):
    step = pl.program_id(0)
    here = proto_ref.shape[1] // LANES

    @pl.when(step == 0)
    def _():
        t = teacher_ref[...].astype(jnp.float32)
        first = lax.axis_index("proto") % 2 == 0
        mine_ref[0] = jnp.where(first, t, student_ref[...].astype(jnp.float32))
        unit[...] = (t * lax.rsqrt(jnp.sum(t * t, 1, keepdims=True) + eps)).astype(jnp.bfloat16)

    for j in range(here):
        span = slice(j * LANES, (j + 1) * LANES)
        w = proto_ref[:, span].astype(jnp.float32)
        gains = gain_ref[pl.ds(step * here + j, 1), :]
        w = (w * lax.rsqrt(jnp.sum(w * w, 0, keepdims=True) + eps) * gains).astype(jnp.bfloat16)
        proto_n_ref[:, span] = w
    e = jnp.exp(jnp.dot(unit[...], proto_n_ref[...], preferred_element_type=jnp.float32) / teacher_temp)
    e = e.astype(jnp.bfloat16)
    cols = proto_ref.shape[1]
    expo_ref[:, pl.ds(pl.multiple_of(step * cols, LANES), cols)] = e
    c = jnp.sum(e.astype(jnp.float32), 0, keepdims=True)
    terms[pl.ds(step, 1), :] = c

    @pl.when(step == pl.num_programs(0) - 1)
    def _():
        sent_ref[...] = jnp.broadcast_to(terms[...][None], sent_ref.shape)


def start(teacher, student, prototypes, gain, peers):
    rows, depth = teacher.shape
    cols = prototypes.shape[1]
    groups = cols // LANES
    steps = HALVES
    chunk = cols // steps
    return pl.pallas_call(
        start_kernel,
        grid=(steps,),
        in_specs=[
            pl.BlockSpec((rows, depth), lambda i: (0, 0)),
            pl.BlockSpec((rows, depth), lambda i: (0, 0)),
            pl.BlockSpec((depth, chunk), lambda i: (0, i)),
            pl.BlockSpec((groups, LANES), lambda i: (0, 0)),
        ],
        out_specs=[
            pl.BlockSpec((1, rows, depth), lambda i: (0, 0, 0)),
            pl.BlockSpec((depth, chunk), lambda i: (0, i)),
            pl.BlockSpec(memory_space=pltpu.VMEM),
            pl.BlockSpec(memory_space=pltpu.VMEM),
        ],
        out_shape=(
            jax.ShapeDtypeStruct((1, rows, depth), jnp.float32),
            jax.ShapeDtypeStruct((depth, cols), jnp.bfloat16),
            pltpu.VMEM((rows, cols), jnp.bfloat16),
            pltpu.VMEM((peers, steps, chunk), jnp.float32),
        ),
        scratch_shapes=[pltpu.VMEM((rows, depth), jnp.bfloat16), pltpu.VMEM((steps, chunk), jnp.float32)],
        compiler_params=pltpu.CompilerParams(vmem_limit_bytes=60 * 2**20),
        cost_estimate=pl.CostEstimate(
            flops=2 * rows * depth * cols, bytes_accessed=6 * depth * cols, transcendentals=rows * cols
        ),
    )(teacher, student, prototypes, gain.reshape(groups, LANES))


def local_call(kernel, operands, waited, out_shape, flops):
    n = len(operands)

    def body(*refs):
        kernel(*refs[:n], *refs[n + len(waited) :])

    return pl.pallas_call(
        body,
        in_specs=[pl.BlockSpec()] * n + [pl.BlockSpec(memory_space=pl.ANY)] * len(waited),
        out_shape=out_shape,
        compiler_params=pltpu.CompilerParams(vmem_limit_bytes=SMALL),
        cost_estimate=pl.CostEstimate(flops=flops, bytes_accessed=flops, transcendentals=0),
    )(*operands, *waited)


def row_kernel(came_ref, expo_ref, *refs):
    total_ref, (sent_ref, u_ref) = (refs[0] if len(refs) == 3 else None), refs[-2:]
    u = 1.0 / jnp.sum(came_ref[...], 0)
    half = u.shape[1] // LANES
    for j in range(u_ref.shape[0]):
        u_ref[j : j + 1, :] = u[j // half : j // half + 1, j % half * LANES : (j % half + 1) * LANES]
    rows = expo_ref.shape[0]
    block = 64
    sums = []
    for first in range(0, rows, block):
        acc = jnp.zeros((block, LANES), jnp.float32)
        for j in range(u_ref.shape[0]):
            e = expo_ref[first : first + block, j * LANES : (j + 1) * LANES].astype(jnp.float32)
            acc += e * u_ref[j : j + 1, :]
        sums.append(acc)
    r = jnp.sum(jnp.concatenate(sums, 0).T, 0, keepdims=True)
    peers = sent_ref.shape[0]
    sent_ref[:, 0:1, :] = jnp.broadcast_to(r[None], (peers, 1, rows))
    if total_ref is not None:
        sent_ref[:, 1:2, :] = jnp.broadcast_to(total_ref[...][None], (peers, 1, rows))


def row_terms(came, expo, peers, *waited, total=None):
    more = () if total is None else (total,)
    rows = expo.shape[0]
    out_shape = (
        jax.ShapeDtypeStruct((peers, 1 + len(more), rows), jnp.float32),
        jax.ShapeDtypeStruct((expo.shape[1] // LANES, LANES), jnp.float32),
    )
    return local_call(row_kernel, (came, expo, *more), waited, out_shape, 2 * expo.size)


def column_kernel(came_ref, expo_ref, sent_ref):
    rows = expo_ref.shape[0]
    v = 1.0 / jnp.sum(came_ref[...], 0)
    v = jnp.broadcast_to(v, (LANES, rows)).T
    peers, halves, cols = sent_ref.shape
    for h in range(halves):
        for first in range(0, cols, LANES):
            e = expo_ref[:, h * cols + first : h * cols + first + LANES].astype(jnp.float32)
            sent_ref[0, h : h + 1, first : first + LANES] = jnp.sum(e * v, 0, keepdims=True)
    sent_ref[1:] = jnp.broadcast_to(sent_ref[0:1], (peers - 1, halves, cols))


def column_terms(came, expo, peers, *waited):
    out_shape = jax.ShapeDtypeStruct((peers, HALVES, expo.shape[1] // HALVES), jnp.float32)
    return local_call(column_kernel, (came, expo), waited, out_shape, 2 * expo.size)


def team_kernel(own_ref, other_ref, proto_ref, u_ref, after_ref, expo_ref, student_exp_ref, student_ref, u_out_ref, proto_t):
    @pl.when(pl.program_id(0) == 0)
    def _():
        start = pl.multiple_of(first_group(proto_ref.shape[1] // LANES) * LANES, LANES)
        proto_t[...] = proto_ref[:, pl.ds(start, HELD * LANES)].astype(jnp.float32).T.astype(jnp.bfloat16)
        u_out_ref[...] = u_ref[...]

    def unit(x):
        return (x * lax.rsqrt(jnp.sum(x * x, 1, keepdims=True) + eps)).astype(jnp.bfloat16)

    across = (((1,), (1,)), ((), ()))
    first = lax.axis_index("proto") % 2 == 0
    proto = proto_t[...]
    t = unit(jnp.where(first, own_ref[0], other_ref[0]))
    s = unit(jnp.where(first, other_ref[0], own_ref[0]))
    student_ref[...] = s
    lt = lax.dot_general(proto, t, across, preferred_element_type=jnp.float32)
    expo_ref[...] = jnp.exp(lt / teacher_temp).astype(jnp.bfloat16)
    ls = lax.dot_general(proto, s, across, preferred_element_type=jnp.float32)
    student_exp_ref[...] = jnp.exp(ls / student_temp)


def team_products(own, other, proto, u, waited):
    senders, rows, depth = own.shape
    part = HELD * LANES
    return pl.pallas_call(
        team_kernel,
        grid=(senders,),
        in_specs=[
            pl.BlockSpec((1, rows, depth), lambda i: (i, 0, 0)),
            pl.BlockSpec((1, rows, depth), lambda i: (i, 0, 0)),
            pl.BlockSpec(proto.shape, lambda i: (0, 0)),
            pl.BlockSpec(u.shape, lambda i: (0, 0)),
            pl.BlockSpec(memory_space=pl.ANY),
        ],
        out_specs=[
            pl.BlockSpec((part, rows), lambda i: (0, i)),
            pl.BlockSpec((part, rows), lambda i: (0, i)),
            pl.BlockSpec((rows, depth), lambda i: (i, 0)),
            pl.BlockSpec(u.shape, lambda i: (0, 0)),
        ],
        out_shape=(
            jax.ShapeDtypeStruct((part, senders * rows), jnp.bfloat16),
            jax.ShapeDtypeStruct((part, senders * rows), jnp.float32),
            jax.ShapeDtypeStruct((senders * rows, depth), jnp.bfloat16),
            jax.ShapeDtypeStruct(u.shape, jnp.float32),
        ),
        scratch_shapes=[pltpu.VMEM((part, depth), jnp.bfloat16)],
        compiler_params=pltpu.CompilerParams(vmem_limit_bytes=TEAM_VMEM),
        cost_estimate=pl.CostEstimate(
            flops=4 * part * senders * rows * depth,
            bytes_accessed=10 * 2**20,
            transcendentals=2 * part * senders * rows,
        ),
    )(own, other, proto, u, waited)


def local(teacher, student, prototypes, gain):
    rows, depth = teacher.shape
    nb, npr = lax.axis_size("batch"), lax.axis_size("proto")
    rows_of_chips = [
        [(t * TEAM + i) * npr + p for i in range(TEAM) for p in range(npr)] for t in range(nb // TEAM)
    ]
    cols = prototypes.shape[1]
    count = cols * npr
    rows_all = rows * nb

    mine, proto_n, expo, sent = start(teacher, student, prototypes, gain, nb)

    def member(rows, flip):
        return lax.ppermute(rows, "batch", [(i, i ^ flip) for i in range(nb)])

    held = [mine, member(mine, 1), None, member(mine, 3)]
    came = lax.all_to_all(sent, "batch", 0, 0, tiled=True)
    sent, _ = row_terms(came, expo, npr, held[1])
    came = lax.all_to_all(sent, "proto", 0, 0, tiled=True)
    sent = column_terms(came, expo, nb, held[3])
    held[2] = member(mine, 2)
    came = lax.all_to_all(sent, "batch", 0, 0, tiled=True)
    sent, _ = row_terms(came, expo, npr, held[2])
    own = jnp.concatenate(held)
    came = lax.all_to_all(sent, "proto", 0, 0, tiled=True)
    sent = column_terms(came, expo, nb)
    other = lax.ppermute(own, "proto", [(i, i ^ 1) for i in range(npr)])
    came = lax.all_to_all(sent, "batch", 0, 0, tiled=True)

    logits = jnp.dot(unit_rows(student), proto_n, preferred_element_type=jnp.float32)
    local_total = jnp.sum(jnp.exp(logits / student_temp), 1)
    sent, scale_u = row_terms(came, expo, TEAM * npr, other, total=local_total[None])
    came = lax.all_to_all(sent, ("batch", "proto"), 0, 0, tiled=True, axis_index_groups=rows_of_chips)
    team_values = team_products(own, other, proto_n, scale_u, sent)

    inv_root = 1.0 / rows_all**0.5
    grad_t, inverse = partial_grad(*team_values, came, float(count), inv_root, nb)
    scale_v = inverse[0]
    parts = lax.all_to_all(grad_t, "batch", 0, 0, tiled=True)
    grad = pl.pallas_call(
        join_kernel,
        out_shape=jax.ShapeDtypeStruct((depth // nb, cols), jnp.float32),
        compiler_params=pltpu.CompilerParams(vmem_limit_bytes=SMALL),
    )(parts)

    scale_u = scale_u.reshape(cols)
    assign = expo.astype(jnp.float32) * scale_u[None, :] * scale_v[:, None]
    targets = (count * assign).astype(jnp.bfloat16)
    return (targets, grad)


def solution(mesh):
    return jax.shard_map(
        local,
        mesh=mesh,
        in_specs=(P("batch", None), P("batch", None), P(None, "proto"), P("proto")),
        out_specs=(P("batch", "proto"), P("batch", "proto")),
        check_vma=False,
    )
```

```python
import functools

import jax
import jax.numpy as jnp
from jax import lax
from jax.experimental import pallas as pl
from jax.experimental.pallas import tpu as pltpu
from jax.sharding import PartitionSpec as P

ITERS = 3
SMALL, VMEM = 16 * 2**20, 61 * 2**20
TEAM_VMEM, GRAD_VMEM = 56 * 2**20, 61 * 2**20
LANES = 128
HELD = 6
SPLIT = 4
HALVES = 2
TEAM = 4


teacher_temp = 0.04
student_temp = 0.1
eps = 1e-06


def unit_rows(x):
    xf = x.astype(jnp.float32)
    return (xf * lax.rsqrt(jnp.sum(xf * xf, 1, keepdims=True) + eps)).astype(jnp.bfloat16)


def first_group(groups):
    return jnp.minimum(lax.axis_index("batch") % TEAM * HELD, groups - HELD)


def grad_kernel(count, scale, *refs):
    exps, student_exps = refs[:SPLIT], refs[SPLIT : 2 * SPLIT]
    student_ref, u_ref, came_ref, out_ref, own_ref, diff = refs[2 * SPLIT :]
    senders = came_ref.shape[0] // TEAM
    rows = came_ref.shape[2]
    chunk = diff.shape[0]
    piece = chunk // SPLIT
    me = lax.axis_index("batch") % TEAM
    u = u_ref[pl.ds(first_group(u_ref.shape[0]) + pl.program_id(0) * (chunk // LANES), chunk // LANES), :]
    wide = [jnp.broadcast_to(u[g : g + 1, :], (LANES, LANES)).T for g in range(chunk // LANES)]
    wide = jnp.concatenate(wide, 0)
    for place in range(TEAM):
        by = 1.0 / jnp.sum(came_ref[pl.ds((me ^ place) * senders, senders)], 0)
        if place == 0:
            own_ref[...] = by
        by = by * count
        for first in range(0, rows, LANES):
            v = by[0:1, first : first + LANES]
            inv_total = by[1:2, first : first + LANES]
            span = slice(place * rows + first, place * rows + first + LANES)
            for i in range(SPLIT):
                part = slice(i * piece, (i + 1) * piece)
                assign = exps[i][:, span].astype(jnp.float32) * wide[part, :] * v
                prob = student_exps[i][:, span] * inv_total
                diff[part, span] = (prob - assign).astype(jnp.bfloat16)
    product = jnp.dot(diff[...], student_ref[...], preferred_element_type=jnp.float32)
    out_ref[...] = (product.T * scale).reshape(out_ref.shape)


def partial_grad(expo_t, student_exp_t, student, u, came, count, scale, owners):
    part, crops = expo_t.shape
    depth = student.shape[1]
    steps = 2
    chunk = part // steps
    piece = chunk // SPLIT

    def pieces():
        return [pl.BlockSpec((piece, crops), lambda i, k=k: (i * SPLIT + k, 0)) for k in range(SPLIT)]

    return pl.pallas_call(
        functools.partial(grad_kernel, count, scale),
        grid=(steps,),
        in_specs=[
            *pieces(),
            *pieces(),
            pl.BlockSpec(student.shape, lambda i: (0, 0)),
            pl.BlockSpec(u.shape, lambda i: (0, 0)),
            pl.BlockSpec(came.shape, lambda i: (0, 0, 0)),
        ],
        out_specs=[
            pl.BlockSpec((owners, depth // owners, chunk), lambda i: (0, 0, i)),
            pl.BlockSpec(came.shape[1:], lambda i: (0, 0)),
        ],
        out_shape=(
            jax.ShapeDtypeStruct((owners, depth // owners, part), jnp.float32),
            jax.ShapeDtypeStruct(came.shape[1:], jnp.float32),
        ),
        scratch_shapes=[pltpu.VMEM((chunk, crops), jnp.bfloat16)],
        compiler_params=pltpu.CompilerParams(vmem_limit_bytes=GRAD_VMEM),
        cost_estimate=pl.CostEstimate(
            flops=2 * part * crops * depth, bytes_accessed=6 * part * crops, transcendentals=0
        ),
    )(*[expo_t] * SPLIT, *[student_exp_t] * SPLIT, student, u, came)


def join_kernel(parts_ref, out_ref):
    teams = parts_ref.shape[0] // TEAM
    groups = out_ref.shape[1] // LANES
    for i in range(TEAM):
        start = min(i * HELD, groups - HELD) * LANES
        total = parts_ref[i]
        for t in range(1, teams):
            total += parts_ref[t * TEAM + i]
        out_ref[:, start : start + HELD * LANES] = total


def start_kernel(teacher_ref, proto_ref, gain_ref, expo_ref, sent_ref, unit, proto_n, terms):
    step = pl.program_id(0)
    here = proto_ref.shape[1] // LANES

    @pl.when(step == 0)
    def _():
        t = teacher_ref[...].astype(jnp.float32)
        unit[...] = (t * lax.rsqrt(jnp.sum(t * t, 1, keepdims=True) + eps)).astype(jnp.bfloat16)

    for j in range(here):
        span = slice(j * LANES, (j + 1) * LANES)
        w = proto_ref[:, span].astype(jnp.float32)
        gains = gain_ref[pl.ds(step * here + j, 1), :]
        w = (w * lax.rsqrt(jnp.sum(w * w, 0, keepdims=True) + eps) * gains).astype(jnp.bfloat16)
        proto_n[:, span] = w
    e = jnp.exp(jnp.dot(unit[...], proto_n[...], preferred_element_type=jnp.float32) / teacher_temp)
    e = e.astype(jnp.bfloat16)
    cols = proto_ref.shape[1]
    expo_ref[:, pl.ds(pl.multiple_of(step * cols, LANES), cols)] = e
    c = jnp.sum(e.astype(jnp.float32), 0, keepdims=True)
    terms[pl.ds(step, 1), :] = c

    @pl.when(step == pl.num_programs(0) - 1)
    def _():
        sent_ref[...] = jnp.broadcast_to(terms[...][None], sent_ref.shape)


def start(teacher, prototypes, gain, peers):
    rows, depth = teacher.shape
    cols = prototypes.shape[1]
    groups = cols // LANES
    steps = HALVES
    chunk = cols // steps
    return pl.pallas_call(
        start_kernel,
        grid=(steps,),
        in_specs=[
            pl.BlockSpec((rows, depth), lambda i: (0, 0)),
            pl.BlockSpec((depth, chunk), lambda i: (0, i)),
            pl.BlockSpec((groups, LANES), lambda i: (0, 0)),
        ],
        out_specs=[
            pl.BlockSpec(memory_space=pltpu.VMEM),
            pl.BlockSpec(memory_space=pltpu.VMEM),
        ],
        out_shape=(
            pltpu.VMEM((rows, cols), jnp.bfloat16),
            pltpu.VMEM((peers, steps, chunk), jnp.float32),
        ),
        scratch_shapes=[
            pltpu.VMEM((rows, depth), jnp.bfloat16),
            pltpu.VMEM((depth, chunk), jnp.bfloat16),
            pltpu.VMEM((steps, chunk), jnp.float32),
        ],
        compiler_params=pltpu.CompilerParams(vmem_limit_bytes=60 * 2**20),
        cost_estimate=pl.CostEstimate(
            flops=2 * rows * depth * cols, bytes_accessed=6 * depth * cols, transcendentals=rows * cols
        ),
    )(teacher, prototypes, gain.reshape(groups, LANES))


def local_call(kernel, operands, waited, out_shape, flops):
    n = len(operands)

    def body(*refs):
        kernel(*refs[:n], *refs[n + len(waited) :])

    return pl.pallas_call(
        body,
        in_specs=[pl.BlockSpec()] * n + [pl.BlockSpec(memory_space=pl.ANY)] * len(waited),
        out_shape=out_shape,
        compiler_params=pltpu.CompilerParams(vmem_limit_bytes=SMALL),
        cost_estimate=pl.CostEstimate(flops=flops, bytes_accessed=flops, transcendentals=0),
    )(*operands, *waited)


def row_kernel(came_ref, expo_ref, *refs):
    total_ref, (sent_ref, u_ref) = (refs[0] if len(refs) == 3 else None), refs[-2:]
    u = 1.0 / jnp.sum(came_ref[...], 0)
    half = u.shape[1] // LANES
    for j in range(u_ref.shape[0]):
        u_ref[j : j + 1, :] = u[j // half : j // half + 1, j % half * LANES : (j % half + 1) * LANES]
    rows = expo_ref.shape[0]
    block = 64
    sums = []
    for first in range(0, rows, block):
        acc = jnp.zeros((block, LANES), jnp.float32)
        for j in range(u_ref.shape[0]):
            e = expo_ref[first : first + block, j * LANES : (j + 1) * LANES].astype(jnp.float32)
            acc += e * u_ref[j : j + 1, :]
        sums.append(acc)
    r = jnp.sum(jnp.concatenate(sums, 0).T, 0, keepdims=True)
    peers = sent_ref.shape[0]
    sent_ref[:, 0:1, :] = jnp.broadcast_to(r[None], (peers, 1, rows))
    if total_ref is not None:
        sent_ref[:, 1:2, :] = jnp.broadcast_to(total_ref[...][None], (peers, 1, rows))


def row_terms(came, expo, peers, *waited, total=None):
    more = () if total is None else (total,)
    rows = expo.shape[0]
    out_shape = (
        pltpu.VMEM((peers, 1 + len(more), rows), jnp.float32),
        jax.ShapeDtypeStruct((expo.shape[1] // LANES, LANES), jnp.float32),
    )
    return local_call(row_kernel, (came, expo, *more), waited, out_shape, 2 * expo.size)


def column_kernel(came_ref, expo_ref, sent_ref):
    rows = expo_ref.shape[0]
    v = 1.0 / jnp.sum(came_ref[...], 0)
    v = jnp.broadcast_to(v, (LANES, rows)).T
    peers, halves, cols = sent_ref.shape
    for h in range(halves):
        for first in range(0, cols, LANES):
            e = expo_ref[:, h * cols + first : h * cols + first + LANES].astype(jnp.float32)
            sent_ref[0, h : h + 1, first : first + LANES] = jnp.sum(e * v, 0, keepdims=True)
    sent_ref[1:] = jnp.broadcast_to(sent_ref[0:1], (peers - 1, halves, cols))


def column_terms(came, expo, peers, *waited):
    out_shape = pltpu.VMEM((peers, HALVES, expo.shape[1] // HALVES), jnp.float32)
    return local_call(column_kernel, (came, expo), waited, out_shape, 2 * expo.size)


def team_kernel(own_ref, other_ref, proto_ref, u_ref, after_ref, expo_ref, student_exp_ref, student_ref, u_out_ref, proto_t):
    @pl.when(pl.program_id(0) == 0)
    def _():
        start = pl.multiple_of(first_group(proto_ref.shape[1] // LANES) * LANES, LANES)
        proto_t[...] = proto_ref[:, pl.ds(start, HELD * LANES)].astype(jnp.float32).T.astype(jnp.bfloat16)
        u_out_ref[...] = u_ref[...]

    def unit(x):
        return (x * lax.rsqrt(jnp.sum(x * x, 1, keepdims=True) + eps)).astype(jnp.bfloat16)

    across = (((1,), (1,)), ((), ()))
    first = lax.axis_index("proto") % 2 == 0
    proto = proto_t[...]
    t = unit(jnp.where(first, own_ref[0], other_ref[0]))
    s = unit(jnp.where(first, other_ref[0], own_ref[0]))
    student_ref[...] = s
    lt = lax.dot_general(proto, t, across, preferred_element_type=jnp.float32)
    expo_ref[...] = jnp.exp(lt / teacher_temp).astype(jnp.bfloat16)
    ls = lax.dot_general(proto, s, across, preferred_element_type=jnp.float32)
    student_exp_ref[...] = jnp.exp(ls / student_temp)


def team_products(own, other, proto, u, waited):
    senders, rows, depth = own.shape
    part = HELD * LANES
    return pl.pallas_call(
        team_kernel,
        grid=(senders,),
        in_specs=[
            pl.BlockSpec((1, rows, depth), lambda i: (i, 0, 0)),
            pl.BlockSpec((1, rows, depth), lambda i: (i, 0, 0)),
            pl.BlockSpec(proto.shape, lambda i: (0, 0)),
            pl.BlockSpec(u.shape, lambda i: (0, 0)),
            pl.BlockSpec(memory_space=pl.ANY),
        ],
        out_specs=[
            pl.BlockSpec((part, rows), lambda i: (0, i)),
            pl.BlockSpec((part, rows), lambda i: (0, i)),
            pl.BlockSpec((rows, depth), lambda i: (i, 0)),
            pl.BlockSpec(u.shape, lambda i: (0, 0)),
        ],
        out_shape=(
            jax.ShapeDtypeStruct((part, senders * rows), jnp.bfloat16),
            jax.ShapeDtypeStruct((part, senders * rows), jnp.float32),
            jax.ShapeDtypeStruct((senders * rows, depth), jnp.bfloat16),
            jax.ShapeDtypeStruct(u.shape, jnp.float32),
        ),
        scratch_shapes=[pltpu.VMEM((part, depth), jnp.bfloat16)],
        compiler_params=pltpu.CompilerParams(vmem_limit_bytes=TEAM_VMEM),
        cost_estimate=pl.CostEstimate(
            flops=4 * part * senders * rows * depth,
            bytes_accessed=10 * 2**20,
            transcendentals=2 * part * senders * rows,
        ),
    )(own, other, proto, u, waited)


def local(teacher, student, prototypes, gain):
    rows, depth = teacher.shape
    nb, npr = lax.axis_size("batch"), lax.axis_size("proto")
    rows_of_chips = [
        [(t * TEAM + i) * npr + p for i in range(TEAM) for p in range(npr)] for t in range(nb // TEAM)
    ]
    cols = prototypes.shape[1]
    count = cols * npr
    rows_all = rows * nb

    expo, sent = start(teacher, prototypes, gain, nb)
    core = lax.axis_index("proto") % 2
    mine = jnp.where(core == 0, teacher.astype(jnp.float32), student.astype(jnp.float32))
    mine = lax.optimization_barrier(mine)[None]
    wf = prototypes.astype(jnp.float32)
    proto_n = (wf * lax.rsqrt(jnp.sum(wf * wf, 0, keepdims=True) + eps) * gain[None, :]).astype(
        jnp.bfloat16
    )

    def member(rows, flip):
        return lax.ppermute(rows, "batch", [(i, i ^ flip) for i in range(nb)])

    held = [mine, member(mine, 1), None, member(mine, 3)]
    came = lax.all_to_all(sent, "batch", 0, 0, tiled=True)
    sent, _ = row_terms(came, expo, npr, held[1])
    came = lax.all_to_all(sent, "proto", 0, 0, tiled=True)
    sent = column_terms(came, expo, nb, held[3])
    held[2] = member(mine, 2)
    came = lax.all_to_all(sent, "batch", 0, 0, tiled=True)
    sent, _ = row_terms(came, expo, npr, held[2])
    own = jnp.concatenate(held)
    came = lax.all_to_all(sent, "proto", 0, 0, tiled=True)
    sent = column_terms(came, expo, nb)
    other = lax.ppermute(own, "proto", [(i, i ^ 1) for i in range(npr)])
    came = lax.all_to_all(sent, "batch", 0, 0, tiled=True)

    logits = jnp.dot(unit_rows(student), proto_n, preferred_element_type=jnp.float32)
    local_total = jnp.sum(jnp.exp(logits / student_temp), 1)
    sent, scale_u = row_terms(came, expo, TEAM * npr, other, total=local_total[None])
    came = lax.all_to_all(sent, ("batch", "proto"), 0, 0, tiled=True, axis_index_groups=rows_of_chips)
    team_values = team_products(own, other, proto_n, scale_u, sent)

    inv_root = 1.0 / rows_all**0.5
    grad_t, inverse = partial_grad(*team_values, came, float(count), inv_root, nb)
    scale_v = inverse[0]
    parts = lax.all_to_all(grad_t, "batch", 0, 0, tiled=True)
    grad = pl.pallas_call(
        join_kernel,
        out_shape=jax.ShapeDtypeStruct((depth // nb, cols), jnp.float32),
        compiler_params=pltpu.CompilerParams(vmem_limit_bytes=SMALL),
    )(parts)

    scale_u = scale_u.reshape(cols)
    assign = expo.astype(jnp.float32) * scale_u[None, :] * scale_v[:, None]
    targets = (count * assign).astype(jnp.bfloat16)
    return (targets, grad)


def solution(mesh):
    return jax.shard_map(
        local,
        mesh=mesh,
        in_specs=(P("batch", None), P("batch", None), P(None, "proto"), P("proto")),
        out_specs=(P("batch", "proto"), P("batch", "proto")),
        check_vma=False,
    )
```

```python
import functools

import jax
import jax.numpy as jnp
from jax import lax
from jax.experimental import pallas as pl
from jax.experimental.pallas import tpu as pltpu
from jax.sharding import PartitionSpec as P

ITERS = 3
SMALL, VMEM = 16 * 2**20, 61 * 2**20
TEAM_VMEM, GRAD_VMEM = 56 * 2**20, 61 * 2**20
LANES = 128
HELD = 6
SPLIT = 4
HALVES = 2
TEAM = 4


teacher_temp = 0.04
student_temp = 0.1
eps = 1e-06


def unit_rows(x):
    xf = x.astype(jnp.float32)
    return (xf * lax.rsqrt(jnp.sum(xf * xf, 1, keepdims=True) + eps)).astype(jnp.bfloat16)


def first_group(groups):
    return jnp.minimum(lax.axis_index("batch") % TEAM * HELD, groups - HELD)


def grad_kernel(count, scale, *refs):
    exps, student_exps = refs[:SPLIT], refs[SPLIT : 2 * SPLIT]
    student_ref, u_ref, came_ref, totals_ref, out_ref, own_ref, diff = refs[2 * SPLIT :]
    senders = came_ref.shape[0] // TEAM
    rows = came_ref.shape[2]
    chunk = diff.shape[0]
    piece = chunk // SPLIT
    me = lax.axis_index("batch") % TEAM
    u = u_ref[pl.ds(first_group(u_ref.shape[0]) + pl.program_id(0) * (chunk // LANES), chunk // LANES), :]
    wide = [jnp.broadcast_to(u[g : g + 1, :], (LANES, LANES)).T for g in range(chunk // LANES)]
    wide = jnp.concatenate(wide, 0)
    for place in range(TEAM):
        by = 1.0 / jnp.sum(came_ref[pl.ds((me ^ place) * senders, senders)], 0)
        if place == 0:
            own_ref[...] = by
        by = by * count
        inv_totals = count / totals_ref[me ^ place]
        for first in range(0, rows, LANES):
            v = by[:, first : first + LANES]
            inv_total = inv_totals[first // LANES : first // LANES + 1, :]
            span = slice(place * rows + first, place * rows + first + LANES)
            for i in range(SPLIT):
                part = slice(i * piece, (i + 1) * piece)
                assign = exps[i][:, span].astype(jnp.float32) * wide[part, :] * v
                prob = student_exps[i][:, span] * inv_total
                diff[part, span] = (prob - assign).astype(jnp.bfloat16)
    product = jnp.dot(diff[...], student_ref[...], preferred_element_type=jnp.float32)
    out_ref[...] = (product.T * scale).reshape(out_ref.shape)


def partial_grad(expo_t, student_exp_t, student, u, came, totals, count, scale, owners):
    part, crops = expo_t.shape
    depth = student.shape[1]
    steps = 2
    chunk = part // steps
    piece = chunk // SPLIT

    def pieces():
        return [pl.BlockSpec((piece, crops), lambda i, k=k: (i * SPLIT + k, 0)) for k in range(SPLIT)]

    return pl.pallas_call(
        functools.partial(grad_kernel, count, scale),
        grid=(steps,),
        in_specs=[
            *pieces(),
            *pieces(),
            pl.BlockSpec(student.shape, lambda i: (0, 0)),
            pl.BlockSpec(u.shape, lambda i: (0, 0)),
            pl.BlockSpec(came.shape, lambda i: (0, 0, 0)),
            pl.BlockSpec(totals.shape, lambda i: (0, 0, 0)),
        ],
        out_specs=[
            pl.BlockSpec((owners, depth // owners, chunk), lambda i: (0, 0, i)),
            pl.BlockSpec(came.shape[1:], lambda i: (0, 0)),
        ],
        out_shape=(
            jax.ShapeDtypeStruct((owners, depth // owners, part), jnp.float32),
            jax.ShapeDtypeStruct(came.shape[1:], jnp.float32),
        ),
        scratch_shapes=[pltpu.VMEM((chunk, crops), jnp.bfloat16)],
        compiler_params=pltpu.CompilerParams(vmem_limit_bytes=GRAD_VMEM),
        cost_estimate=pl.CostEstimate(
            flops=2 * part * crops * depth, bytes_accessed=6 * part * crops, transcendentals=0
        ),
    )(*[expo_t] * SPLIT, *[student_exp_t] * SPLIT, student, u, came, totals)


def join_kernel(parts_ref, out_ref):
    teams = parts_ref.shape[0] // TEAM
    groups = out_ref.shape[1] // LANES
    for i in range(TEAM):
        start = min(i * HELD, groups - HELD) * LANES
        total = parts_ref[i]
        for t in range(1, teams):
            total += parts_ref[t * TEAM + i]
        out_ref[:, start : start + HELD * LANES] = total


def start_kernel(teacher_ref, student_ref, proto_ref, gain_ref, mine_ref, proto_n_ref, expo_ref, sent_ref, unit, terms):
    step = pl.program_id(0)
    here = proto_ref.shape[1] // LANES

    @pl.when(step == 0)
    def _():
        t = teacher_ref[...].astype(jnp.float32)
        first = lax.axis_index("proto") % 2 == 0
        mine_ref[0] = jnp.where(first, t, student_ref[...].astype(jnp.float32))
        unit[...] = (t * lax.rsqrt(jnp.sum(t * t, 1, keepdims=True) + eps)).astype(jnp.bfloat16)

    for j in range(here):
        span = slice(j * LANES, (j + 1) * LANES)
        w = proto_ref[:, span].astype(jnp.float32)
        gains = gain_ref[pl.ds(step * here + j, 1), :]
        w = (w * lax.rsqrt(jnp.sum(w * w, 0, keepdims=True) + eps) * gains).astype(jnp.bfloat16)
        proto_n_ref[:, span] = w
    e = jnp.exp(jnp.dot(unit[...], proto_n_ref[...], preferred_element_type=jnp.float32) / teacher_temp)
    e = e.astype(jnp.bfloat16)
    cols = proto_ref.shape[1]
    expo_ref[:, pl.ds(pl.multiple_of(step * cols, LANES), cols)] = e
    c = jnp.sum(e.astype(jnp.float32), 0, keepdims=True)
    terms[pl.ds(step, 1), :] = c

    @pl.when(step == pl.num_programs(0) - 1)
    def _():
        sent_ref[...] = jnp.broadcast_to(terms[...][None], sent_ref.shape)


def start(teacher, student, prototypes, gain, peers):
    rows, depth = teacher.shape
    cols = prototypes.shape[1]
    groups = cols // LANES
    steps = HALVES
    chunk = cols // steps
    return pl.pallas_call(
        start_kernel,
        grid=(steps,),
        in_specs=[
            pl.BlockSpec((rows, depth), lambda i: (0, 0)),
            pl.BlockSpec((rows, depth), lambda i: (0, 0)),
            pl.BlockSpec((depth, chunk), lambda i: (0, i)),
            pl.BlockSpec((groups, LANES), lambda i: (0, 0)),
        ],
        out_specs=[
            pl.BlockSpec((1, rows, depth), lambda i: (0, 0, 0)),
            pl.BlockSpec((depth, chunk), lambda i: (0, i)),
            pl.BlockSpec(memory_space=pltpu.VMEM),
            pl.BlockSpec(memory_space=pltpu.VMEM),
        ],
        out_shape=(
            jax.ShapeDtypeStruct((1, rows, depth), jnp.float32),
            jax.ShapeDtypeStruct((depth, cols), jnp.bfloat16),
            pltpu.VMEM((rows, cols), jnp.bfloat16),
            pltpu.VMEM((peers, steps, chunk), jnp.float32),
        ),
        scratch_shapes=[pltpu.VMEM((rows, depth), jnp.bfloat16), pltpu.VMEM((steps, chunk), jnp.float32)],
        compiler_params=pltpu.CompilerParams(vmem_limit_bytes=60 * 2**20),
        cost_estimate=pl.CostEstimate(
            flops=2 * rows * depth * cols, bytes_accessed=6 * depth * cols, transcendentals=rows * cols
        ),
    )(teacher, student, prototypes, gain.reshape(groups, LANES))


def local_call(kernel, operands, waited, out_shape, flops):
    n = len(operands)

    def body(*refs):
        kernel(*refs[:n], *refs[n + len(waited) :])

    return pl.pallas_call(
        body,
        in_specs=[pl.BlockSpec()] * n + [pl.BlockSpec(memory_space=pl.ANY)] * len(waited),
        out_shape=out_shape,
        compiler_params=pltpu.CompilerParams(vmem_limit_bytes=SMALL),
        cost_estimate=pl.CostEstimate(flops=flops, bytes_accessed=flops, transcendentals=0),
    )(*operands, *waited)


def row_kernel(has_total, came_ref, expo_ref, *refs):
    total_ref = refs[0] if has_total else None
    sent_ref, u_ref, *team_ref = refs[1:] if has_total else refs
    groups = u_ref.shape[0]
    half = groups // HALVES
    u = 1.0 / jnp.sum(came_ref[:, :, : half * LANES], 0)
    for j in range(groups):
        u_ref[j : j + 1, :] = u[j // half : j // half + 1, j % half * LANES : (j % half + 1) * LANES]
    if team_ref:
        first = lax.axis_index("batch") // TEAM * TEAM
        team_ref[0][...] = came_ref[pl.ds(first, TEAM), :, half * LANES :]
    rows = expo_ref.shape[0]
    block = 64
    sums = []
    for first in range(0, rows, block):
        acc = jnp.zeros((block, LANES), jnp.float32)
        for j in range(groups):
            e = expo_ref[first : first + block, j * LANES : (j + 1) * LANES].astype(jnp.float32)
            acc += e * u_ref[j : j + 1, :]
        sums.append(acc)
    r = jnp.sum(jnp.concatenate(sums, 0).T, 0, keepdims=True)
    peers = sent_ref.shape[0]
    sent_ref[:, 0:1, :] = jnp.broadcast_to(r[None], (peers, 1, rows))
    if has_total:
        sent_ref[:, 1:2, :] = jnp.broadcast_to(total_ref[...][None], (peers, 1, rows))


def row_terms(came, expo, peers, *waited, total=None):
    more = () if total is None else (total,)
    rows, cols = expo.shape
    extra = came.shape[2] - cols // HALVES
    out_shape = (
        jax.ShapeDtypeStruct((peers, 1 + len(more), rows), jnp.float32),
        jax.ShapeDtypeStruct((cols // LANES, LANES), jnp.float32),
    )
    if extra:
        out_shape += (jax.ShapeDtypeStruct((TEAM, HALVES, extra), jnp.float32),)
    kernel = functools.partial(row_kernel, bool(more))
    return local_call(kernel, (came, expo, *more), waited, out_shape, 2 * expo.size)


def column_kernel(came_ref, expo_ref, sent_ref):
    rows = expo_ref.shape[0]
    got = jnp.sum(came_ref[...], 0)
    v = jnp.broadcast_to(1.0 / got[0:1], (LANES, rows)).T
    peers, halves, width = sent_ref.shape
    cols = expo_ref.shape[1] // halves
    for h in range(halves):
        for first in range(0, cols, LANES):
            e = expo_ref[:, h * cols + first : h * cols + first + LANES].astype(jnp.float32)
            sent_ref[0, h : h + 1, first : first + LANES] = jnp.sum(e * v, 0, keepdims=True)
    if width > cols:
        for h in range(halves):
            sent_ref[0, h : h + 1, cols:] = got[1:2, h * (width - cols) : (h + 1) * (width - cols)]
    sent_ref[1:] = jnp.broadcast_to(sent_ref[0:1], (peers - 1, halves, width))


def column_terms(came, expo, peers, *waited):
    extra = (came.shape[1] - 1) * came.shape[2]
    out_shape = jax.ShapeDtypeStruct((peers, HALVES, (expo.shape[1] + extra) // HALVES), jnp.float32)
    return local_call(column_kernel, (came, expo), waited, out_shape, 2 * expo.size)


def team_kernel(own_ref, other_ref, proto_ref, u_ref, after_ref, expo_ref, student_exp_ref, student_ref, u_out_ref, proto_t):
    @pl.when(pl.program_id(0) == 0)
    def _():
        start = pl.multiple_of(first_group(proto_ref.shape[1] // LANES) * LANES, LANES)
        proto_t[...] = proto_ref[:, pl.ds(start, HELD * LANES)].astype(jnp.float32).T.astype(jnp.bfloat16)
        u_out_ref[...] = u_ref[...]

    def unit(x):
        return (x * lax.rsqrt(jnp.sum(x * x, 1, keepdims=True) + eps)).astype(jnp.bfloat16)

    across = (((1,), (1,)), ((), ()))
    first = lax.axis_index("proto") % 2 == 0
    proto = proto_t[...]
    t = unit(jnp.where(first, own_ref[0], other_ref[0]))
    s = unit(jnp.where(first, other_ref[0], own_ref[0]))
    student_ref[...] = s
    lt = lax.dot_general(proto, t, across, preferred_element_type=jnp.float32)
    expo_ref[...] = jnp.exp(lt / teacher_temp).astype(jnp.bfloat16)
    ls = lax.dot_general(proto, s, across, preferred_element_type=jnp.float32)
    student_exp_ref[...] = jnp.exp(ls / student_temp)


def team_products(own, other, proto, u, waited):
    senders, rows, depth = own.shape
    part = HELD * LANES
    return pl.pallas_call(
        team_kernel,
        grid=(senders,),
        in_specs=[
            pl.BlockSpec((1, rows, depth), lambda i: (i, 0, 0)),
            pl.BlockSpec((1, rows, depth), lambda i: (i, 0, 0)),
            pl.BlockSpec(proto.shape, lambda i: (0, 0)),
            pl.BlockSpec(u.shape, lambda i: (0, 0)),
            pl.BlockSpec(memory_space=pl.ANY),
        ],
        out_specs=[
            pl.BlockSpec((part, rows), lambda i: (0, i)),
            pl.BlockSpec((part, rows), lambda i: (0, i)),
            pl.BlockSpec((rows, depth), lambda i: (i, 0)),
            pl.BlockSpec(u.shape, lambda i: (0, 0)),
        ],
        out_shape=(
            jax.ShapeDtypeStruct((part, senders * rows), jnp.bfloat16),
            jax.ShapeDtypeStruct((part, senders * rows), jnp.float32),
            jax.ShapeDtypeStruct((senders * rows, depth), jnp.bfloat16),
            jax.ShapeDtypeStruct(u.shape, jnp.float32),
        ),
        scratch_shapes=[pltpu.VMEM((part, depth), jnp.bfloat16)],
        compiler_params=pltpu.CompilerParams(vmem_limit_bytes=TEAM_VMEM),
        cost_estimate=pl.CostEstimate(
            flops=4 * part * senders * rows * depth,
            bytes_accessed=10 * 2**20,
            transcendentals=2 * part * senders * rows,
        ),
    )(own, other, proto, u, waited)


def local(teacher, student, prototypes, gain):
    rows, depth = teacher.shape
    nb, npr = lax.axis_size("batch"), lax.axis_size("proto")
    rows_of_chips = [
        [(t * TEAM + i) * npr + p for i in range(TEAM) for p in range(npr)] for t in range(nb // TEAM)
    ]
    cols = prototypes.shape[1]
    count = cols * npr
    rows_all = rows * nb

    mine, proto_n, expo, sent = start(teacher, student, prototypes, gain, nb)

    logits = jnp.dot(unit_rows(student), proto_n, preferred_element_type=jnp.float32)
    local_total = jnp.sum(jnp.exp(logits / student_temp), 1)

    def member(rows, flip):
        return lax.ppermute(rows, "batch", [(i, i ^ flip) for i in range(nb)])

    held = [mine, member(mine, 1), None, member(mine, 3)]
    came = lax.all_to_all(sent, "batch", 0, 0, tiled=True)
    sent, _ = row_terms(came, expo, npr, held[1])
    came = lax.all_to_all(sent, "proto", 0, 0, tiled=True)
    sent = column_terms(came, expo, nb, held[3])
    held[2] = member(mine, 2)
    came = lax.all_to_all(sent, "batch", 0, 0, tiled=True)
    sent, _ = row_terms(came, expo, npr, held[2], total=local_total[None])
    own = jnp.concatenate(held)
    came = lax.all_to_all(sent, "proto", 0, 0, tiled=True)
    sent = column_terms(came, expo, nb)
    other = lax.ppermute(own, "proto", [(i, i ^ 1) for i in range(npr)])
    came = lax.all_to_all(sent, "batch", 0, 0, tiled=True)

    sent, scale_u, totals = row_terms(came, expo, TEAM * npr, other)
    came = lax.all_to_all(sent, ("batch", "proto"), 0, 0, tiled=True, axis_index_groups=rows_of_chips)
    team_values = team_products(own, other, proto_n, scale_u, sent)

    inv_root = 1.0 / rows_all**0.5
    grad_t, inverse = partial_grad(*team_values, came, totals, float(count), inv_root, nb)
    scale_v = inverse[0]
    parts = lax.all_to_all(grad_t, "batch", 0, 0, tiled=True)
    grad = pl.pallas_call(
        join_kernel,
        out_shape=jax.ShapeDtypeStruct((depth // nb, cols), jnp.float32),
        compiler_params=pltpu.CompilerParams(vmem_limit_bytes=SMALL),
    )(parts)

    scale_u = scale_u.reshape(cols)
    assign = expo.astype(jnp.float32) * scale_u[None, :] * scale_v[:, None]
    targets = (count * assign).astype(jnp.bfloat16)
    return (targets, grad)


def solution(mesh):
    return jax.shard_map(
        local,
        mesh=mesh,
        in_specs=(P("batch", None), P("batch", None), P(None, "proto"), P("proto")),
        out_specs=(P("batch", "proto"), P("batch", "proto")),
        check_vma=False,
    )
```

```python
import functools

import jax
import jax.numpy as jnp
from jax import lax
from jax.experimental import pallas as pl
from jax.experimental.pallas import tpu as pltpu
from jax.sharding import PartitionSpec as P

ITERS = 3
SMALL, VMEM = 16 * 2**20, 61 * 2**20
TEAM_VMEM, GRAD_VMEM = 50 * 2**20, 61 * 2**20
LANES = 128
HELD = 6
SPLIT = 4
HALVES = 2
TEAM = 4


teacher_temp = 0.04
student_temp = 0.1
eps = 1e-06


def unit_rows(x):
    xf = x.astype(jnp.float32)
    return (xf * lax.rsqrt(jnp.sum(xf * xf, 1, keepdims=True) + eps)).astype(jnp.bfloat16)


def first_group(groups):
    return jnp.minimum(lax.axis_index("batch") % TEAM * HELD, groups - HELD)


def grad_kernel(count, scale, *refs):
    exps, student_exps = refs[:SPLIT], refs[SPLIT : 2 * SPLIT]
    student_ref, u_ref, came_ref, totals_ref, out_ref, own_ref, diff = refs[2 * SPLIT :]
    senders = came_ref.shape[0] // TEAM
    rows = came_ref.shape[2]
    chunk = diff.shape[0]
    piece = chunk // SPLIT
    me = lax.axis_index("batch") % TEAM
    u = u_ref[pl.ds(first_group(u_ref.shape[0]) + pl.program_id(0) * (chunk // LANES), chunk // LANES), :]
    wide = [jnp.broadcast_to(u[g : g + 1, :], (LANES, LANES)).T for g in range(chunk // LANES)]
    wide = jnp.concatenate(wide, 0)
    for place in range(TEAM):
        by = 1.0 / jnp.sum(came_ref[pl.ds((me ^ place) * senders, senders)], 0)
        if place == 0:
            own_ref[...] = by
        by = by * count
        inv_totals = count / totals_ref[me ^ place]
        for first in range(0, rows, LANES):
            v = by[:, first : first + LANES]
            inv_total = inv_totals[first // LANES : first // LANES + 1, :]
            span = slice(place * rows + first, place * rows + first + LANES)
            for i in range(SPLIT):
                part = slice(i * piece, (i + 1) * piece)
                assign = exps[i][:, span].astype(jnp.float32) * wide[part, :] * v
                prob = student_exps[i][:, span] * inv_total
                diff[part, span] = (prob - assign).astype(jnp.bfloat16)
    product = jnp.dot(diff[...], student_ref[...], preferred_element_type=jnp.float32)
    out_ref[...] = (product.T * scale).reshape(out_ref.shape)


def partial_grad(expo_t, student_exp_t, student, u, came, totals, count, scale, owners):
    part, crops = expo_t.shape
    depth = student.shape[1]
    steps = 2
    chunk = part // steps
    piece = chunk // SPLIT

    def pieces():
        return [pl.BlockSpec((piece, crops), lambda i, k=k: (i * SPLIT + k, 0)) for k in range(SPLIT)]

    return pl.pallas_call(
        functools.partial(grad_kernel, count, scale),
        grid=(steps,),
        in_specs=[
            *pieces(),
            *pieces(),
            pl.BlockSpec(student.shape, lambda i: (0, 0)),
            pl.BlockSpec(u.shape, lambda i: (0, 0)),
            pl.BlockSpec(came.shape, lambda i: (0, 0, 0)),
            pl.BlockSpec(totals.shape, lambda i: (0, 0, 0)),
        ],
        out_specs=[
            pl.BlockSpec((owners, depth // owners, chunk), lambda i: (0, 0, i)),
            pl.BlockSpec(came.shape[1:], lambda i: (0, 0)),
        ],
        out_shape=(
            jax.ShapeDtypeStruct((owners, depth // owners, part), jnp.float32),
            jax.ShapeDtypeStruct(came.shape[1:], jnp.float32),
        ),
        scratch_shapes=[pltpu.VMEM((chunk, crops), jnp.bfloat16)],
        compiler_params=pltpu.CompilerParams(vmem_limit_bytes=GRAD_VMEM),
        cost_estimate=pl.CostEstimate(
            flops=2 * part * crops * depth, bytes_accessed=6 * part * crops, transcendentals=0
        ),
    )(*[expo_t] * SPLIT, *[student_exp_t] * SPLIT, student, u, came, totals)


def join_kernel(parts_ref, out_ref):
    teams = parts_ref.shape[0] // TEAM
    groups = out_ref.shape[1] // LANES
    for i in range(TEAM):
        start = min(i * HELD, groups - HELD) * LANES
        total = parts_ref[i]
        for t in range(1, teams):
            total += parts_ref[t * TEAM + i]
        out_ref[:, start : start + HELD * LANES] = total


def start_kernel(teacher_ref, student_ref, proto_ref, gain_ref, mine_ref, proto_n_ref, expo_ref, sent_ref, unit, terms):
    step = pl.program_id(0)
    here = proto_ref.shape[1] // LANES

    @pl.when(step == 0)
    def _():
        t = teacher_ref[...].astype(jnp.float32)
        first = lax.axis_index("proto") % 2 == 0
        mine_ref[0] = jnp.where(first, t, student_ref[...].astype(jnp.float32))
        unit[...] = (t * lax.rsqrt(jnp.sum(t * t, 1, keepdims=True) + eps)).astype(jnp.bfloat16)

    for j in range(here):
        span = slice(j * LANES, (j + 1) * LANES)
        w = proto_ref[:, span].astype(jnp.float32)
        gains = gain_ref[pl.ds(step * here + j, 1), :]
        w = (w * lax.rsqrt(jnp.sum(w * w, 0, keepdims=True) + eps) * gains).astype(jnp.bfloat16)
        proto_n_ref[:, span] = w
    e = jnp.exp(jnp.dot(unit[...], proto_n_ref[...], preferred_element_type=jnp.float32) / teacher_temp)
    e = e.astype(jnp.bfloat16)
    cols = proto_ref.shape[1]
    expo_ref[:, pl.ds(pl.multiple_of(step * cols, LANES), cols)] = e
    c = jnp.sum(e.astype(jnp.float32), 0, keepdims=True)
    terms[pl.ds(step, 1), :] = c

    @pl.when(step == pl.num_programs(0) - 1)
    def _():
        sent_ref[...] = jnp.broadcast_to(terms[...][None], sent_ref.shape)


def start(teacher, student, prototypes, gain, peers):
    rows, depth = teacher.shape
    cols = prototypes.shape[1]
    groups = cols // LANES
    steps = HALVES
    chunk = cols // steps
    return pl.pallas_call(
        start_kernel,
        grid=(steps,),
        in_specs=[
            pl.BlockSpec((rows, depth), lambda i: (0, 0)),
            pl.BlockSpec((rows, depth), lambda i: (0, 0)),
            pl.BlockSpec((depth, chunk), lambda i: (0, i)),
            pl.BlockSpec((groups, LANES), lambda i: (0, 0)),
        ],
        out_specs=[
            pl.BlockSpec((1, rows, depth), lambda i: (0, 0, 0)),
            pl.BlockSpec((depth, chunk), lambda i: (0, i)),
            pl.BlockSpec(memory_space=pltpu.VMEM),
            pl.BlockSpec(memory_space=pltpu.VMEM),
        ],
        out_shape=(
            jax.ShapeDtypeStruct((1, rows, depth), jnp.float32),
            jax.ShapeDtypeStruct((depth, cols), jnp.bfloat16),
            pltpu.VMEM((rows, cols), jnp.bfloat16),
            pltpu.VMEM((peers, steps, chunk), jnp.float32),
        ),
        scratch_shapes=[pltpu.VMEM((rows, depth), jnp.bfloat16), pltpu.VMEM((steps, chunk), jnp.float32)],
        compiler_params=pltpu.CompilerParams(vmem_limit_bytes=60 * 2**20),
        cost_estimate=pl.CostEstimate(
            flops=2 * rows * depth * cols, bytes_accessed=6 * depth * cols, transcendentals=rows * cols
        ),
    )(teacher, student, prototypes, gain.reshape(groups, LANES))


def local_call(kernel, operands, waited, out_shape, flops):
    n = len(operands)

    def body(*refs):
        kernel(*refs[:n], *refs[n + len(waited) :])

    return pl.pallas_call(
        body,
        in_specs=[pl.BlockSpec()] * n + [pl.BlockSpec(memory_space=pl.ANY)] * len(waited),
        out_shape=out_shape,
        compiler_params=pltpu.CompilerParams(vmem_limit_bytes=SMALL),
        cost_estimate=pl.CostEstimate(flops=flops, bytes_accessed=flops, transcendentals=0),
    )(*operands, *waited)


def row_kernel(has_total, came_ref, expo_ref, *refs):
    total_ref = refs[0] if has_total else None
    sent_ref, u_ref, *team_ref = refs[1:] if has_total else refs
    groups = u_ref.shape[0]
    half = groups // HALVES
    u = 1.0 / jnp.sum(came_ref[:, :, : half * LANES], 0)
    for j in range(groups):
        u_ref[j : j + 1, :] = u[j // half : j // half + 1, j % half * LANES : (j % half + 1) * LANES]
    if team_ref:
        first = lax.axis_index("batch") // TEAM * TEAM
        team_ref[0][...] = came_ref[pl.ds(first, TEAM), :, half * LANES :]
    rows = expo_ref.shape[0]
    block = 64
    sums = []
    for first in range(0, rows, block):
        acc = jnp.zeros((block, LANES), jnp.float32)
        for j in range(groups):
            e = expo_ref[first : first + block, j * LANES : (j + 1) * LANES].astype(jnp.float32)
            acc += e * u_ref[j : j + 1, :]
        sums.append(acc)
    r = jnp.sum(jnp.concatenate(sums, 0).T, 0, keepdims=True)
    peers = sent_ref.shape[0]
    sent_ref[:, 0:1, :] = jnp.broadcast_to(r[None], (peers, 1, rows))
    if has_total:
        sent_ref[:, 1:2, :] = jnp.broadcast_to(total_ref[...][None], (peers, 1, rows))


def row_terms(came, expo, peers, *waited, total=None):
    more = () if total is None else (total,)
    rows, cols = expo.shape
    extra = came.shape[2] - cols // HALVES
    out_shape = (
        jax.ShapeDtypeStruct((peers, 1 + len(more), rows), jnp.float32),
        jax.ShapeDtypeStruct((cols // LANES, LANES), jnp.float32),
    )
    if extra:
        out_shape += (jax.ShapeDtypeStruct((TEAM, HALVES, extra), jnp.float32),)
    kernel = functools.partial(row_kernel, bool(more))
    return local_call(kernel, (came, expo, *more), waited, out_shape, 2 * expo.size)


def column_kernel(came_ref, expo_ref, sent_ref):
    rows = expo_ref.shape[0]
    got = jnp.sum(came_ref[...], 0)
    v = jnp.broadcast_to(1.0 / got[0:1], (LANES, rows)).T
    peers, halves, width = sent_ref.shape
    cols = expo_ref.shape[1] // halves
    for h in range(halves):
        for first in range(0, cols, LANES):
            e = expo_ref[:, h * cols + first : h * cols + first + LANES].astype(jnp.float32)
            sent_ref[0, h : h + 1, first : first + LANES] = jnp.sum(e * v, 0, keepdims=True)
    if width > cols:
        for h in range(halves):
            sent_ref[0, h : h + 1, cols:] = got[1:2, h * (width - cols) : (h + 1) * (width - cols)]
    sent_ref[1:] = jnp.broadcast_to(sent_ref[0:1], (peers - 1, halves, width))


def column_terms(came, expo, peers, *waited):
    extra = (came.shape[1] - 1) * came.shape[2]
    out_shape = jax.ShapeDtypeStruct((peers, HALVES, (expo.shape[1] + extra) // HALVES), jnp.float32)
    return local_call(column_kernel, (came, expo), waited, out_shape, 2 * expo.size)


def team_kernel(own_ref, other_ref, proto_ref, u_ref, after_ref, expo_ref, student_exp_ref, student_ref, u_out_ref, proto_t):
    @pl.when(pl.program_id(0) == 0)
    def _():
        start = pl.multiple_of(first_group(proto_ref.shape[1] // LANES) * LANES, LANES)
        proto_t[...] = proto_ref[:, pl.ds(start, HELD * LANES)].astype(jnp.float32).T.astype(jnp.bfloat16)
        u_out_ref[...] = u_ref[...]

    def unit(x):
        return (x * lax.rsqrt(jnp.sum(x * x, 1, keepdims=True) + eps)).astype(jnp.bfloat16)

    across = (((1,), (1,)), ((), ()))
    first = lax.axis_index("proto") % 2 == 0
    proto = proto_t[...]
    t = unit(jnp.where(first, own_ref[0], other_ref[0]))
    s = unit(jnp.where(first, other_ref[0], own_ref[0]))
    student_ref[...] = s
    lt = lax.dot_general(proto, t, across, preferred_element_type=jnp.float32)
    expo_ref[...] = jnp.exp(lt / teacher_temp).astype(jnp.bfloat16)
    ls = lax.dot_general(proto, s, across, preferred_element_type=jnp.float32)
    student_exp_ref[...] = jnp.exp(ls / student_temp)


def team_products(own, other, proto, u, waited):
    senders, rows, depth = own.shape
    part = HELD * LANES
    return pl.pallas_call(
        team_kernel,
        grid=(senders,),
        in_specs=[
            pl.BlockSpec((1, rows, depth), lambda i: (i, 0, 0)),
            pl.BlockSpec((1, rows, depth), lambda i: (i, 0, 0)),
            pl.BlockSpec(proto.shape, lambda i: (0, 0)),
            pl.BlockSpec(u.shape, lambda i: (0, 0)),
            pl.BlockSpec(memory_space=pl.ANY),
        ],
        out_specs=[
            pl.BlockSpec((part, rows), lambda i: (0, i)),
            pl.BlockSpec((part, rows), lambda i: (0, i)),
            pl.BlockSpec((rows, depth), lambda i: (i, 0)),
            pl.BlockSpec(u.shape, lambda i: (0, 0)),
        ],
        out_shape=(
            jax.ShapeDtypeStruct((part, senders * rows), jnp.bfloat16),
            jax.ShapeDtypeStruct((part, senders * rows), jnp.float32),
            jax.ShapeDtypeStruct((senders * rows, depth), jnp.bfloat16),
            jax.ShapeDtypeStruct(u.shape, jnp.float32),
        ),
        scratch_shapes=[pltpu.VMEM((part, depth), jnp.bfloat16)],
        compiler_params=pltpu.CompilerParams(vmem_limit_bytes=TEAM_VMEM),
        cost_estimate=pl.CostEstimate(
            flops=4 * part * senders * rows * depth,
            bytes_accessed=10 * 2**20,
            transcendentals=2 * part * senders * rows,
        ),
    )(own, other, proto, u, waited)


def local(teacher, student, prototypes, gain):
    rows, depth = teacher.shape
    nb, npr = lax.axis_size("batch"), lax.axis_size("proto")
    rows_of_chips = [
        [(t * TEAM + i) * npr + p for i in range(TEAM) for p in range(npr)] for t in range(nb // TEAM)
    ]
    cols = prototypes.shape[1]
    count = cols * npr
    rows_all = rows * nb

    mine, proto_n, expo, sent = start(teacher, student, prototypes, gain, nb)

    logits = jnp.dot(unit_rows(student), proto_n, preferred_element_type=jnp.float32)
    local_total = jnp.sum(jnp.exp(logits / student_temp), 1)

    def member(rows, flip):
        return lax.ppermute(rows, "batch", [(i, i ^ flip) for i in range(nb)])

    held = [mine, member(mine, 1), None, member(mine, 3)]
    came = lax.all_to_all(sent, "batch", 0, 0, tiled=True)
    sent, _ = row_terms(came, expo, npr, held[1])
    came = lax.all_to_all(sent, "proto", 0, 0, tiled=True)
    sent = column_terms(came, expo, nb, held[3])
    held[2] = member(mine, 2)
    came = lax.all_to_all(sent, "batch", 0, 0, tiled=True)
    sent, _ = row_terms(came, expo, npr, held[2], total=local_total[None])
    own = jnp.concatenate(held)
    came = lax.all_to_all(sent, "proto", 0, 0, tiled=True)
    sent = column_terms(came, expo, nb)
    other = lax.ppermute(own, "proto", [(i, i ^ 1) for i in range(npr)])
    came = lax.all_to_all(sent, "batch", 0, 0, tiled=True)

    sent, scale_u, totals = row_terms(came, expo, TEAM * npr, other)
    came = lax.all_to_all(sent, ("batch", "proto"), 0, 0, tiled=True, axis_index_groups=rows_of_chips)
    team_values = team_products(own, other, proto_n, scale_u, sent)

    inv_root = 1.0 / rows_all**0.5
    grad_t, inverse = partial_grad(*team_values, came, totals, float(count), inv_root, nb)
    scale_v = inverse[0]
    parts = lax.all_to_all(grad_t, "batch", 0, 0, tiled=True)
    grad = pl.pallas_call(
        join_kernel,
        out_shape=jax.ShapeDtypeStruct((depth // nb, cols), jnp.float32),
        compiler_params=pltpu.CompilerParams(vmem_limit_bytes=SMALL),
    )(parts)

    scale_u = scale_u.reshape(cols)
    assign = expo.astype(jnp.float32) * scale_u[None, :] * scale_v[:, None]
    targets = (count * assign).astype(jnp.bfloat16)
    return (targets, grad)


def solution(mesh):
    return jax.shard_map(
        local,
        mesh=mesh,
        in_specs=(P("batch", None), P("batch", None), P(None, "proto"), P("proto")),
        out_specs=(P("batch", "proto"), P("batch", "proto")),
        check_vma=False,
    )
```

```python
import functools

import jax
import jax.numpy as jnp
from jax import lax
from jax.experimental import pallas as pl
from jax.experimental.pallas import tpu as pltpu
from jax.sharding import PartitionSpec as P

ITERS = 3
SMALL, VMEM = 16 * 2**20, 61 * 2**20
TEAM_VMEM, GRAD_VMEM = 50 * 2**20, 52 * 2**20
LANES = 128
HELD = 6
SPLIT = 4
HALVES = 2
TEAM = 4


teacher_temp = 0.04
student_temp = 0.1
eps = 1e-06


def unit_rows(x):
    xf = x.astype(jnp.float32)
    return (xf * lax.rsqrt(jnp.sum(xf * xf, 1, keepdims=True) + eps)).astype(jnp.bfloat16)


def first_group(groups):
    return jnp.minimum(lax.axis_index("batch") % TEAM * HELD, groups - HELD)


def grad_kernel(count, scale, *refs):
    exps, student_exps = refs[:SPLIT], refs[SPLIT : 2 * SPLIT]
    student_ref, u_ref, came_ref, totals_ref, out_ref, own_ref, diff = refs[2 * SPLIT :]
    senders = came_ref.shape[0] // TEAM
    rows = came_ref.shape[2]
    chunk = diff.shape[0]
    piece = chunk // SPLIT
    me = lax.axis_index("batch") % TEAM
    u = u_ref[pl.ds(first_group(u_ref.shape[0]) + pl.program_id(0) * (chunk // LANES), chunk // LANES), :]
    wide = [jnp.broadcast_to(u[g : g + 1, :], (LANES, LANES)).T for g in range(chunk // LANES)]
    wide = jnp.concatenate(wide, 0)
    for place in range(TEAM):
        by = 1.0 / jnp.sum(came_ref[pl.ds((me ^ place) * senders, senders)], 0)
        if place == 0:
            own_ref[...] = by
        by = by * count
        inv_totals = count / totals_ref[me ^ place]
        for first in range(0, rows, LANES):
            v = by[:, first : first + LANES]
            inv_total = inv_totals[first // LANES : first // LANES + 1, :]
            span = slice(place * rows + first, place * rows + first + LANES)
            for i in range(SPLIT):
                part = slice(i * piece, (i + 1) * piece)
                assign = exps[i][:, span].astype(jnp.float32) * wide[part, :] * v
                prob = student_exps[i][:, span] * inv_total
                diff[part, span] = (prob - assign).astype(jnp.bfloat16)
    product = jnp.dot(diff[...], student_ref[...], preferred_element_type=jnp.float32)
    out_ref[...] = (product.T * scale).reshape(out_ref.shape)


def partial_grad(expo_t, student_exp_t, student, u, came, totals, count, scale, owners):
    part, crops = expo_t.shape
    depth = student.shape[1]
    steps = 2
    chunk = part // steps
    piece = chunk // SPLIT

    def pieces():
        return [pl.BlockSpec((piece, crops), lambda i, k=k: (i * SPLIT + k, 0)) for k in range(SPLIT)]

    return pl.pallas_call(
        functools.partial(grad_kernel, count, scale),
        grid=(steps,),
        in_specs=[
            *pieces(),
            *pieces(),
            pl.BlockSpec(student.shape, lambda i: (0, 0)),
            pl.BlockSpec(u.shape, lambda i: (0, 0)),
            pl.BlockSpec(came.shape, lambda i: (0, 0, 0)),
            pl.BlockSpec(totals.shape, lambda i: (0, 0, 0)),
        ],
        out_specs=[
            pl.BlockSpec((owners, depth // owners, chunk), lambda i: (0, 0, i)),
            pl.BlockSpec(came.shape[1:], lambda i: (0, 0)),
        ],
        out_shape=(
            jax.ShapeDtypeStruct((owners, depth // owners, part), jnp.float32),
            jax.ShapeDtypeStruct(came.shape[1:], jnp.float32),
        ),
        scratch_shapes=[pltpu.VMEM((chunk, crops), jnp.bfloat16)],
        compiler_params=pltpu.CompilerParams(vmem_limit_bytes=GRAD_VMEM),
        cost_estimate=pl.CostEstimate(
            flops=2 * part * crops * depth, bytes_accessed=6 * part * crops, transcendentals=0
        ),
    )(*[expo_t] * SPLIT, *[student_exp_t] * SPLIT, student, u, came, totals)


def join_kernel(parts_ref, out_ref):
    teams = parts_ref.shape[0] // TEAM
    groups = out_ref.shape[1] // LANES
    for i in range(TEAM):
        start = min(i * HELD, groups - HELD) * LANES
        total = parts_ref[i]
        for t in range(1, teams):
            total += parts_ref[t * TEAM + i]
        out_ref[:, start : start + HELD * LANES] = total


def start_kernel(teacher_ref, student_ref, proto_ref, gain_ref, mine_ref, proto_n_ref, expo_ref, sent_ref, unit, terms):
    step = pl.program_id(0)
    here = proto_ref.shape[1] // LANES

    @pl.when(step == 0)
    def _():
        t = teacher_ref[...].astype(jnp.float32)
        first = lax.axis_index("proto") % 2 == 0
        mine_ref[0] = jnp.where(first, t, student_ref[...].astype(jnp.float32))
        unit[...] = (t * lax.rsqrt(jnp.sum(t * t, 1, keepdims=True) + eps)).astype(jnp.bfloat16)

    for j in range(here):
        span = slice(j * LANES, (j + 1) * LANES)
        w = proto_ref[:, span].astype(jnp.float32)
        gains = gain_ref[pl.ds(step * here + j, 1), :]
        w = (w * lax.rsqrt(jnp.sum(w * w, 0, keepdims=True) + eps) * gains).astype(jnp.bfloat16)
        proto_n_ref[:, span] = w
    e = jnp.exp(jnp.dot(unit[...], proto_n_ref[...], preferred_element_type=jnp.float32) / teacher_temp)
    e = e.astype(jnp.bfloat16)
    cols = proto_ref.shape[1]
    expo_ref[:, pl.ds(pl.multiple_of(step * cols, LANES), cols)] = e
    c = jnp.sum(e.astype(jnp.float32), 0, keepdims=True)
    terms[pl.ds(step, 1), :] = c

    @pl.when(step == pl.num_programs(0) - 1)
    def _():
        sent_ref[...] = jnp.broadcast_to(terms[...][None], sent_ref.shape)


def start(teacher, student, prototypes, gain, peers):
    rows, depth = teacher.shape
    cols = prototypes.shape[1]
    groups = cols // LANES
    steps = HALVES
    chunk = cols // steps
    return pl.pallas_call(
        start_kernel,
        grid=(steps,),
        in_specs=[
            pl.BlockSpec((rows, depth), lambda i: (0, 0)),
            pl.BlockSpec((rows, depth), lambda i: (0, 0)),
            pl.BlockSpec((depth, chunk), lambda i: (0, i)),
            pl.BlockSpec((groups, LANES), lambda i: (0, 0)),
        ],
        out_specs=[
            pl.BlockSpec((1, rows, depth), lambda i: (0, 0, 0)),
            pl.BlockSpec((depth, chunk), lambda i: (0, i)),
            pl.BlockSpec(memory_space=pltpu.VMEM),
            pl.BlockSpec(memory_space=pltpu.VMEM),
        ],
        out_shape=(
            jax.ShapeDtypeStruct((1, rows, depth), jnp.float32),
            jax.ShapeDtypeStruct((depth, cols), jnp.bfloat16),
            pltpu.VMEM((rows, cols), jnp.bfloat16),
            pltpu.VMEM((peers, steps, chunk), jnp.float32),
        ),
        scratch_shapes=[pltpu.VMEM((rows, depth), jnp.bfloat16), pltpu.VMEM((steps, chunk), jnp.float32)],
        compiler_params=pltpu.CompilerParams(vmem_limit_bytes=60 * 2**20),
        cost_estimate=pl.CostEstimate(
            flops=2 * rows * depth * cols, bytes_accessed=6 * depth * cols, transcendentals=rows * cols
        ),
    )(teacher, student, prototypes, gain.reshape(groups, LANES))


def local_call(kernel, operands, waited, out_shape, flops):
    n = len(operands)

    def body(*refs):
        kernel(*refs[:n], *refs[n + len(waited) :])

    return pl.pallas_call(
        body,
        in_specs=[pl.BlockSpec()] * n + [pl.BlockSpec(memory_space=pl.ANY)] * len(waited),
        out_shape=out_shape,
        compiler_params=pltpu.CompilerParams(vmem_limit_bytes=SMALL),
        cost_estimate=pl.CostEstimate(flops=flops, bytes_accessed=flops, transcendentals=0),
    )(*operands, *waited)


def row_kernel(has_total, came_ref, expo_ref, *refs):
    total_ref = refs[0] if has_total else None
    sent_ref, u_ref, *team_ref = refs[1:] if has_total else refs
    groups = u_ref.shape[0]
    half = groups // HALVES
    u = 1.0 / jnp.sum(came_ref[:, :, : half * LANES], 0)
    for j in range(groups):
        u_ref[j : j + 1, :] = u[j // half : j // half + 1, j % half * LANES : (j % half + 1) * LANES]
    if team_ref:
        first = lax.axis_index("batch") // TEAM * TEAM
        team_ref[0][...] = came_ref[pl.ds(first, TEAM), :, half * LANES :]
    rows = expo_ref.shape[0]
    block = 64
    sums = []
    for first in range(0, rows, block):
        acc = jnp.zeros((block, LANES), jnp.float32)
        for j in range(groups):
            e = expo_ref[first : first + block, j * LANES : (j + 1) * LANES].astype(jnp.float32)
            acc += e * u_ref[j : j + 1, :]
        sums.append(acc)
    r = jnp.sum(jnp.concatenate(sums, 0).T, 0, keepdims=True)
    peers = sent_ref.shape[0]
    sent_ref[:, 0:1, :] = jnp.broadcast_to(r[None], (peers, 1, rows))
    if has_total:
        sent_ref[:, 1:2, :] = jnp.broadcast_to(total_ref[...][None], (peers, 1, rows))


def row_terms(came, expo, peers, *waited, total=None):
    more = () if total is None else (total,)
    rows, cols = expo.shape
    extra = came.shape[2] - cols // HALVES
    out_shape = (
        jax.ShapeDtypeStruct((peers, 1 + len(more), rows), jnp.float32),
        jax.ShapeDtypeStruct((cols // LANES, LANES), jnp.float32),
    )
    if extra:
        out_shape += (jax.ShapeDtypeStruct((TEAM, HALVES, extra), jnp.float32),)
    kernel = functools.partial(row_kernel, bool(more))
    return local_call(kernel, (came, expo, *more), waited, out_shape, 2 * expo.size)


def column_kernel(came_ref, expo_ref, sent_ref):
    rows = expo_ref.shape[0]
    got = jnp.sum(came_ref[...], 0)
    v = jnp.broadcast_to(1.0 / got[0:1], (LANES, rows)).T
    peers, halves, width = sent_ref.shape
    cols = expo_ref.shape[1] // halves
    for h in range(halves):
        for first in range(0, cols, LANES):
            e = expo_ref[:, h * cols + first : h * cols + first + LANES].astype(jnp.float32)
            sent_ref[0, h : h + 1, first : first + LANES] = jnp.sum(e * v, 0, keepdims=True)
    if width > cols:
        for h in range(halves):
            sent_ref[0, h : h + 1, cols:] = got[1:2, h * (width - cols) : (h + 1) * (width - cols)]
    sent_ref[1:] = jnp.broadcast_to(sent_ref[0:1], (peers - 1, halves, width))


def column_terms(came, expo, peers, *waited):
    extra = (came.shape[1] - 1) * came.shape[2]
    out_shape = jax.ShapeDtypeStruct((peers, HALVES, (expo.shape[1] + extra) // HALVES), jnp.float32)
    return local_call(column_kernel, (came, expo), waited, out_shape, 2 * expo.size)


def team_kernel(own_ref, other_ref, proto_ref, u_ref, after_ref, expo_ref, student_exp_ref, student_ref, u_out_ref, proto_t):
    @pl.when(pl.program_id(0) == 0)
    def _():
        start = pl.multiple_of(first_group(proto_ref.shape[1] // LANES) * LANES, LANES)
        proto_t[...] = proto_ref[:, pl.ds(start, HELD * LANES)].astype(jnp.float32).T.astype(jnp.bfloat16)
        u_out_ref[...] = u_ref[...]

    def unit(x):
        return (x * lax.rsqrt(jnp.sum(x * x, 1, keepdims=True) + eps)).astype(jnp.bfloat16)

    across = (((1,), (1,)), ((), ()))
    first = lax.axis_index("proto") % 2 == 0
    proto = proto_t[...]
    t = unit(jnp.where(first, own_ref[0], other_ref[0]))
    s = unit(jnp.where(first, other_ref[0], own_ref[0]))
    student_ref[...] = s
    lt = lax.dot_general(proto, t, across, preferred_element_type=jnp.float32)
    expo_ref[...] = jnp.exp(lt / teacher_temp).astype(jnp.bfloat16)
    ls = lax.dot_general(proto, s, across, preferred_element_type=jnp.float32)
    student_exp_ref[...] = jnp.exp(ls / student_temp)


def team_products(own, other, proto, u, waited):
    senders, rows, depth = own.shape
    part = HELD * LANES
    return pl.pallas_call(
        team_kernel,
        grid=(senders,),
        in_specs=[
            pl.BlockSpec((1, rows, depth), lambda i: (i, 0, 0)),
            pl.BlockSpec((1, rows, depth), lambda i: (i, 0, 0)),
            pl.BlockSpec(proto.shape, lambda i: (0, 0)),
            pl.BlockSpec(u.shape, lambda i: (0, 0)),
            pl.BlockSpec(memory_space=pl.ANY),
        ],
        out_specs=[
            pl.BlockSpec((part, rows), lambda i: (0, i)),
            pl.BlockSpec((part, rows), lambda i: (0, i)),
            pl.BlockSpec((rows, depth), lambda i: (i, 0)),
            pl.BlockSpec(u.shape, lambda i: (0, 0)),
        ],
        out_shape=(
            jax.ShapeDtypeStruct((part, senders * rows), jnp.bfloat16),
            jax.ShapeDtypeStruct((part, senders * rows), jnp.float32),
            jax.ShapeDtypeStruct((senders * rows, depth), jnp.bfloat16),
            jax.ShapeDtypeStruct(u.shape, jnp.float32),
        ),
        scratch_shapes=[pltpu.VMEM((part, depth), jnp.bfloat16)],
        compiler_params=pltpu.CompilerParams(vmem_limit_bytes=TEAM_VMEM),
        cost_estimate=pl.CostEstimate(
            flops=4 * part * senders * rows * depth,
            bytes_accessed=10 * 2**20,
            transcendentals=2 * part * senders * rows,
        ),
    )(own, other, proto, u, waited)


def local(teacher, student, prototypes, gain):
    rows, depth = teacher.shape
    nb, npr = lax.axis_size("batch"), lax.axis_size("proto")
    rows_of_chips = [
        [(t * TEAM + i) * npr + p for i in range(TEAM) for p in range(npr)] for t in range(nb // TEAM)
    ]
    cols = prototypes.shape[1]
    count = cols * npr
    rows_all = rows * nb

    mine, proto_n, expo, sent = start(teacher, student, prototypes, gain, nb)

    logits = jnp.dot(unit_rows(student), proto_n, preferred_element_type=jnp.float32)
    local_total = jnp.sum(jnp.exp(logits / student_temp), 1)

    def member(rows, flip):
        return lax.ppermute(rows, "batch", [(i, i ^ flip) for i in range(nb)])

    held = [mine, member(mine, 1), None, member(mine, 3)]
    came = lax.all_to_all(sent, "batch", 0, 0, tiled=True)
    sent, _ = row_terms(came, expo, npr, held[1])
    came = lax.all_to_all(sent, "proto", 0, 0, tiled=True)
    sent = column_terms(came, expo, nb, held[3])
    held[2] = member(mine, 2)
    came = lax.all_to_all(sent, "batch", 0, 0, tiled=True)
    sent, _ = row_terms(came, expo, npr, held[2], total=local_total[None])
    own = jnp.concatenate(held)
    came = lax.all_to_all(sent, "proto", 0, 0, tiled=True)
    sent = column_terms(came, expo, nb)
    other = lax.ppermute(own, "proto", [(i, i ^ 1) for i in range(npr)])
    came = lax.all_to_all(sent, "batch", 0, 0, tiled=True)

    sent, scale_u, totals = row_terms(came, expo, TEAM * npr, other)
    came = lax.all_to_all(sent, ("batch", "proto"), 0, 0, tiled=True, axis_index_groups=rows_of_chips)
    team_values = team_products(own, other, proto_n, scale_u, sent)

    inv_root = 1.0 / rows_all**0.5
    grad_t, inverse = partial_grad(*team_values, came, totals, float(count), inv_root, nb)
    scale_v = inverse[0]
    parts = lax.all_to_all(grad_t, "batch", 0, 0, tiled=True)
    grad = pl.pallas_call(
        join_kernel,
        out_shape=jax.ShapeDtypeStruct((depth // nb, cols), jnp.float32),
        compiler_params=pltpu.CompilerParams(vmem_limit_bytes=SMALL),
    )(parts)

    scale_u = scale_u.reshape(cols)
    assign = expo.astype(jnp.float32) * scale_u[None, :] * scale_v[:, None]
    targets = (count * assign).astype(jnp.bfloat16)
    return (targets, grad)


def solution(mesh):
    return jax.shard_map(
        local,
        mesh=mesh,
        in_specs=(P("batch", None), P("batch", None), P(None, "proto"), P("proto")),
        out_specs=(P("batch", "proto"), P("batch", "proto")),
        check_vma=False,
    )
```
